128 devices in a mesh: edge: 16 (over y, z), node: 8 (over x, core).
Axes of the slice: x: 4, y: 4, z: 4, core: 2. Of those that a mesh axis runs over, the one named last changes fastest.
Arguments:
- residual: float32 [64, 131072], P(None, ('edge', 'node')), may hold values from -6 to 6
- tangent: float32 [3, 64, 131072], P(None, None, ('edge', 'node')), may hold values from -4 to 4
- jacobi: float32 [64, 131072], P(None, ('edge', 'node')), may hold values from 0.2 to 1
- ends: int32 [2, 64, 131072], P(None, None, ('edge', 'node')), may hold values from 0 to 31, as said below
- target: int32 [131072, 1], P(('edge', 'node')), may hold values from 0 to 127; in each aligned block of 1024 rows (0 to 1023, 1024 to 2047, ...) at most 16 rows name the same one
- node_block: int32 [131072], P(('edge', 'node')), may hold values from 0 to 1023
- sigma: float32 [512, 32, 256], P(('edge', 'node')), may hold values from 0.25 to 8
Outputs:
- correction: float32 [64, 131072], P(None, ('edge', 'node'))
The draws below stay inside these ranges and needn't reach their ends.
Inputs may be any that keep to these rules, and one draw needn't show every extreme that they name: `ends`: the head and tail of an edge differ. `target`: among the 1024 rows of one device no device is named more than 16 times, and one is named exactly 16 times.
All inputs are finite; a program needn't handle non-finite values.
Results may differ from the reference program's by a relative error of at most 0.000086.
Values sent between devices are 32-bit elements; how exact they have to be, the bound alone decides.
No kernel may reach another device: no remote copies, remote signals or barrier semaphores. Data moves between devices by JAX's collectives and lax.ppermute only.
A program may use at most 64 MiB of HBM per device.

```python
import math
import jax
import jax.numpy as jnp
import numpy as np

BLOCK_EDGES = 64
NODE_BLOCK = 32
R = 32
Z = 256
NBD = 1024
EBD = 1024
CAP = 16
EBLOCKS = 131072
NA = 512
N_EDGE = 16
N_NODE = 8


def draw_ends(key, part):
    key = jax.random.fold_in(key, 11)
    first_key, second_key = jax.random.split(key)
    tail_end = jax.random.randint(first_key, (BLOCK_EDGES, EBLOCKS), 0, NODE_BLOCK)
    offset = jax.random.randint(second_key, (BLOCK_EDGES, EBLOCKS), 1, NODE_BLOCK)
    head_end = (tail_end + offset) % NODE_BLOCK
    return jnp.stack([tail_end, head_end], axis=0).astype(jnp.int32)


def touch_ends(entries, rng, least, top_value):
    spot = [jax.random.randint(jax.random.fold_in(rng, axis), (), 0, length) for axis, length in enumerate(entries.shape)]
    main_axis = entries.shape.index(max(entries.shape))
    beside = spot[:main_axis] + [(spot[main_axis] + 1) % entries.shape[main_axis]] + spot[main_axis + 1:]
    return entries.at[tuple(spot)].set(least).at[tuple(beside)].set(top_value)


def block_scale(own_key, shape, shards, least, largest):
    gain = 1.0
    for position, blocks in shards:
        draws = jax.random.uniform(jax.random.fold_in(jax.random.fold_in(own_key, 6), position), (blocks,), jnp.float32, least / len(shards), largest / len(shards))
        gain = gain * jnp.repeat(jnp.exp(draws), shape[position] // blocks).reshape((-1,) + (1,) * (len(shape) - 1 - position))
    return gain


def assign_block(key, own, number, rows, amount, top, bound, skew):
    sequence = jax.random.permutation(key, amount)
    heavy_load, common = portions_of(amount, rows * top, bound, skew, True), portions_of(amount, rows * top, bound, skew, False)
    places = jnp.arange(amount)

    def named(lengths, rotation):
        used = int((lengths > 0).sum())
        fixed = max(1, used // 4)
        moved = fixed + (places - fixed + rotation * (used - fixed)) % max(1, amount - fixed)
        return jnp.zeros((amount,), jnp.int32).at[sequence[jnp.where(places < fixed, places, moved)]].set(jnp.asarray(lengths, jnp.int32))

    lengths = jnp.where(number % 4 == 0, named(heavy_load, number // 4), named(common, number - number // 4 - 1))
    mixed = jax.random.permutation(jax.random.fold_in(own, 3), amount)
    source_of, receiver = mixed[0:amount // 2 * 2:2], mixed[1:amount // 2 * 2:2]
    room = jnp.minimum(lengths[source_of] - 1, bound - lengths[receiver]) // 2
    room = jnp.where((source_of == sequence[0]) | (receiver == sequence[0]) | (lengths[receiver] == 0), 0, jnp.maximum(room, 0))
    moved = jax.random.randint(jax.random.fold_in(own, 4), (amount // 2,), 0, 1 << 20) % (room + 1)
    lengths = lengths.at[source_of].add(-moved).at[receiver].add(moved)
    members = jnp.searchsorted(jnp.cumsum(lengths), jnp.arange(rows * top), side="right").astype(jnp.int32)
    listing = members.reshape(top, rows).T
    listing = listing[jax.random.permutation(jax.random.fold_in(own, 1), rows)]
    rotation = jax.random.randint(jax.random.fold_in(own, 2), (rows, 1), 0, top)
    return jnp.take_along_axis(listing, (jnp.arange(top)[None, :] + rotation) % top, axis=1)


def portions_of(number_of, total, limit, skew, full):
    loads = [(1 << 20) // math.isqrt(standing ** skew) + 1 for standing in range(1, number_of + 1)]
    largest = limit if full else min(limit, max(-(-total // number_of), total * loads[0] // sum(loads)))
    least = 1 if total - largest >= number_of - 1 else 0
    given, spare = [largest] + [least] * (number_of - 1), total - largest - least * (number_of - 1)
    while spare > 0:
        free = [i for i in range(1, number_of) if given[i] < largest] or [i for i in range(1, number_of) if given[i] < limit]
        mass, budget = sum([loads[i] for i in free]), spare
        for i in free:
            addition = min(limit - given[i], max(1, budget * loads[i] // mass), spare)
            given[i] = given[i] + addition
            spare = spare - addition
    return np.array(given)


def scatter_about(own_key, dims, deviation, bound, cuts=(), kind=jnp.bfloat16):
    drawn = jax.random.normal(own_key, dims, jnp.float32) * deviation
    if len(cuts) > 0:
        drawn = block_scale(own_key, dims, cuts, -0.22, 0.18) * drawn
    return jnp.clip(drawn, min=-bound, max=bound).astype(kind)


def setup_inputs(seed: int = 0) -> dict:
    arg_keys = jax.random.split(jax.random.key(seed), 8)
    residual = scatter_about(arg_keys[0], (BLOCK_EDGES, EBLOCKS), 1.0, 6.0, ((1, 128),), jnp.float32)
    tangent = scatter_about(arg_keys[1], (3, BLOCK_EDGES, EBLOCKS), 0.6, 4.0, ((2, 128),), jnp.float32)
    jacobi = jnp.clip(jnp.exp(math.log(1.0) - 1.609438 * jax.random.uniform(arg_keys[2], (BLOCK_EDGES, EBLOCKS), jnp.float32) ** block_scale(arg_keys[2], (BLOCK_EDGES, EBLOCKS), ((1, 128),), -0.2, 0.2)), 0.2, 1.0)
    ends = draw_ends(jax.random.fold_in(arg_keys[7], 71), 0)
    target_keys = jax.random.split(jax.random.fold_in(arg_keys[4], 1), EBLOCKS // EBD)
    target_turns = jax.random.permutation(jax.random.fold_in(arg_keys[4], 3), EBLOCKS // EBD)
    target = jax.vmap(lambda own, number: assign_block(jax.random.fold_in(arg_keys[4], 2), own, number, EBD, N_EDGE * N_NODE, 1, CAP, 2))(target_keys, target_turns).reshape((EBLOCKS, 1))
    node_block = touch_ends(jax.random.randint(arg_keys[5], (EBLOCKS,), 0, NBD), jax.random.fold_in(arg_keys[5], 1), 0, NBD - 1).astype(jnp.int32)
    sigma = jnp.clip(jnp.exp(math.log(8.0) - 3.465736 * jax.random.uniform(arg_keys[6], (NA, R, Z), jnp.float32) ** block_scale(arg_keys[6], (NA, R, Z), ((0, 128),), -0.2, 0.2)), 0.25, 8.0)
    return dict(residual=residual, tangent=tangent, jacobi=jacobi, ends=ends, target=target, node_block=node_block, sigma=sigma)


mass_scale = (1.0, 1.0, 1.0, 0.5)


def chebyshev_terms():
    scale = jnp.array(mass_scale, jnp.float32).reshape(4, 1, 1, 1)
    upper = 12.0 + 8.0 * scale
    lower = upper / 8.0
    centre = (upper + lower) / 2.0
    radius = (upper - lower) / 2.0
    ratio = centre / radius
    first = 1.0 / ratio
    second = 1.0 / (2.0 * ratio - first)
    return scale, centre, second * first, 2.0 * second / radius


def stiffness(padded, diag):
    centre = padded[:, 1:-1]
    beside_all = padded[:, :-2] + padded[:, 2:]
    inner = jnp.pad(centre, ((0, 0), (0, 0), (1, 1), (1, 1)))
    beside_all = beside_all + inner[:, :, :-2, 1:-1] + inner[:, :, 2:, 1:-1]
    beside_all = beside_all + inner[:, :, 1:-1, :-2] + inner[:, :, 1:-1, 2:]
    return diag * centre - beside_all


def wrapped(field):
    return jnp.concatenate([field[:, -1:], field, field[:, :1]], axis=1)


def reference(residual, tangent, jacobi, ends, target, node_block, sigma):
    scale, centre, coef_one, coef_two = chebyshev_terms()
    global_block = target[:, 0] * NBD + node_block
    base = global_block * NODE_BLOCK
    tail_node = (base[None, :] + ends[0]).reshape(-1)
    head_node = (base[None, :] + ends[1]).reshape(-1)
    node_count = NA * R * Z
    vector_terms = (0.5 * tangent * residual[None]).reshape(3, -1)
    flat_res = residual.reshape(-1)
    nodal_rhs = jnp.zeros((4, node_count), jnp.float32)
    nodal_rhs = nodal_rhs.at[:3, head_node].add(vector_terms)
    nodal_rhs = nodal_rhs.at[:3, tail_node].add(vector_terms)
    nodal_rhs = nodal_rhs.at[3, head_node].add(flat_res)
    nodal_rhs = nodal_rhs.at[3, tail_node].add(-flat_res)
    source = nodal_rhs.reshape(4, NA, R, Z)
    diag = 6.0 + scale * sigma[None]

    def apply(field):
        return stiffness(wrapped(field), diag)

    step_one = source / centre
    rest = source - apply(step_one)
    step_two = coef_one * step_one + coef_two * rest
    solution = step_one + step_two
    rest = source - apply(solution)
    step_one = rest / centre
    rest = rest - apply(step_one)
    step_two = coef_one * step_one + coef_two * rest
    solution = (solution + step_one) + step_two
    flat_sol = solution.reshape(4, -1)
    at_head = flat_sol[:, head_node].reshape(4, BLOCK_EDGES, -1)
    at_tail = flat_sol[:, tail_node].reshape(4, BLOCK_EDGES, -1)
    lifted = 0.5 * jnp.sum(tangent * (at_head[:3] + at_tail[:3]), axis=0)
    return jacobi * residual + lifted + (at_head[3] - at_tail[3])
```

```python
import jax
import jax.numpy as jnp
from jax import lax
from jax.experimental import pallas as pl
from jax.experimental.pallas import tpu as pltpu
from jax.sharding import PartitionSpec as P

F32 = jnp.float32
BF16 = jnp.bfloat16
I32 = jnp.int32

EDGES = 64
NODES = 32
ROW = 4 * NODES
BLOCKS = 1024
CAP = 16
DEVICES = 128
SLOTS = DEVICES * CAP
SLICE = 256
HALO = 3 * SLICE
LABEL = 3 * NODES
RING = ("edge", "node")
VMEM_LIMIT = 48 * 1024 * 1024

mass_scale = (1.0, 1.0, 1.0, 0.5)


def chebyshev_numbers(scale):
    upper = 12.0 + 8.0 * scale
    lower = upper / 8.0
    centre = (upper + lower) / 2.0
    radius = (upper - lower) / 2.0
    ratio = centre / radius
    first = 1.0 / ratio
    second = 1.0 / (2.0 * ratio - first)
    return (centre, second * first, 2.0 * second / radius)


def place(slab):
    return slab ^ (24 * ((slab >> 5) & 1)) ^ (6 * ((slab >> 3) & 1))


def split(value):
    high = value.astype(BF16)
    return high, (value - high.astype(F32)).astype(BF16)


def one_hot(mask):
    return jnp.where(mask, 1.0, 0.0).astype(BF16)


def iota(shape, dim):
    return lax.broadcasted_iota(I32, shape, dim)


def dot(left, right, dims):
    return lax.dot_general(left, right, (dims, ((), ())), preferred_element_type=F32)


def terms_kernel(res_ref, tan_ref, ends_ref, target_ref, block_ref, send_ref, slot_ref, term_scr, acc_scr, hot_scr):
    term_scr[...] = 0.5 * tan_ref[...] * res_ref[...][None]
    node = iota((NODES, 128), 0)

    def lanes_step(group, _):
        lanes = pl.ds(pl.multiple_of(group * 128, 128), 128)

        sums = [jnp.zeros((NODES, 128), F32)] * 4
        for number in range(EDGES):
            edge = slice(number, number + 1)
            head = ends_ref[1, edge, lanes] == node
            tail = ends_ref[0, edge, lanes] == node
            either = head | tail
            value = res_ref[edge, lanes]
            for channel in range(3):
                sums[channel] = sums[channel] + jnp.where(either, term_scr[channel, edge, lanes], 0.0)
            sums[3] = sums[3] + jnp.where(head, value, jnp.where(tail, -value, 0.0))
        for channel in range(4):
            acc_scr[channel * NODES : (channel + 1) * NODES, lanes] = sums[channel]
        return 0

    lax.fori_loop(0, BLOCKS // 128, lanes_step, 0)

    number = block_ref[...]
    label = (number & ~255) + (number & 7) * 32 + ((number >> 3) & 31)
    acc_scr[LABEL : LABEL + 1, :] = (label + 1).astype(F32)

    holder = place(target_ref[...])
    device = iota((DEVICES, 128), 0)
    before = one_hot(iota((128, 128), 0) < iota((128, 128), 1))
    seen = jnp.zeros((DEVICES, 1), F32)
    for group in range(BLOCKS // 128):
        lanes = slice(group * 128, (group + 1) * 128)
        same = holder[:, lanes] == device
        hot = jnp.where(same, 1.0, 0.0)
        count = dot(hot.astype(BF16), before, ((1,), (0,))) + seen
        rank = jnp.sum(jnp.where(same, count, 0.0), axis=0, keepdims=True)
        slot_ref[:, lanes] = holder[:, lanes] * CAP + rank.astype(I32)
        seen = seen + jnp.sum(hot, axis=1, keepdims=True)

    high, low = split(acc_scr[...])
    hot_scr[0:ROW, :] = high
    hot_scr[ROW:, :] = low
    slots = slot_ref[...]

    def send_step(step, _):
        rows = pl.ds(pl.multiple_of(step * 256, 256), 256)
        hot = one_hot(slots == iota((256, BLOCKS), 0) + step * 256)
        both = dot(hot, hot_scr[...], ((1,), (1,)))
        send_ref[rows, :] = both[:, :ROW] + both[:, ROW:]
        return 0

    lax.fori_loop(0, SLOTS // 256, send_step, 0)


def edge_terms(residual, tangent, ends, target, node_block):
    return pl.pallas_call(
        terms_kernel,
        out_shape=(
            jax.ShapeDtypeStruct((SLOTS, ROW), F32),
            jax.ShapeDtypeStruct((1, BLOCKS), I32),
        ),
        in_specs=[pl.BlockSpec(memory_space=pltpu.VMEM)] * 5,
        out_specs=[pl.BlockSpec(memory_space=pltpu.VMEM)] * 2,
        scratch_shapes=[
            pltpu.VMEM((3, EDGES, BLOCKS), F32),
            pltpu.VMEM((ROW, BLOCKS), F32),
            pltpu.VMEM((2 * ROW, BLOCKS), BF16),
        ],
        compiler_params=pltpu.CompilerParams(vmem_limit_bytes=VMEM_LIMIT),
        name="edge_terms",
    )(residual, tangent, ends, target, node_block)


def transposed_rows(rows_ref, out_scr):
    for step in range(SLOTS // 128):
        part = slice(step * 128, (step + 1) * 128)
        high, low = split(rows_ref[part, :].T)
        out_scr[0:ROW, part] = high
        out_scr[ROW:, part] = low


def sums_kernel(got_ref, own_ref, before_ref, after_ref, rows_scr, hot_scr):
    transposed_rows(got_ref, rows_scr)

    def hot_step(step, _):
        part = pl.ds(pl.multiple_of(step * 256, 256), 256)
        label = got_ref[part, LABEL : LABEL + 1].astype(I32)
        hot_scr[part, :] = one_hot(label == iota((256, BLOCKS), 1) + 1)
        return 0

    lax.fori_loop(0, SLOTS // 256, hot_step, 0)
    for step in range(BLOCKS // 256):
        lanes = slice(step * 256, (step + 1) * 256)
        both = dot(rows_scr[...], hot_scr[:, lanes], ((1,), (0,)))
        sums = both[:ROW] + both[ROW:]
        scalar = sums[LABEL:]
        first = iota((NODES, 256), 0) == 0
        rest = -jnp.sum(jnp.where(first, 0.0, scalar), axis=0, keepdims=True)
        own_ref[0:LABEL, lanes] = sums[:LABEL]
        own_ref[LABEL:, lanes] = jnp.where(first, rest, scalar)
    before_ref[...] = own_ref[:, 0:HALO]
    after_ref[...] = own_ref[:, BLOCKS - HALO :]


def block_sums(got):
    return pl.pallas_call(
        sums_kernel,
        out_shape=(
            jax.ShapeDtypeStruct((ROW, BLOCKS), F32),
            jax.ShapeDtypeStruct((ROW, HALO), F32),
            jax.ShapeDtypeStruct((ROW, HALO), F32),
        ),
        in_specs=[pl.BlockSpec(memory_space=pltpu.VMEM)],
        out_specs=[pl.BlockSpec(memory_space=pltpu.VMEM)] * 3,
        scratch_shapes=[
            pltpu.VMEM((2 * ROW, SLOTS), BF16),
            pltpu.VMEM((SLOTS, BLOCKS), BF16),
        ],
        compiler_params=pltpu.CompilerParams(vmem_limit_bytes=VMEM_LIMIT),
        name="block_sums",
    )(got)


def beside(field):
    row = iota((8, SLICE), 0)
    lane = iota((8, SLICE), 1)
    up = pltpu.roll(field, 1, 0)
    edge = up[0:8]
    wrap = jnp.where(lane >= 32, pltpu.roll(edge, 32, 1), 0.0)
    up = jnp.concatenate([jnp.where(row == 0, wrap, edge), up[8:]], axis=0)
    down = pltpu.roll(field, NODES - 1, 0)
    edge = down[24:32]
    wrap = jnp.where(lane < SLICE - 32, pltpu.roll(edge, SLICE - 32, 1), 0.0)
    down = jnp.concatenate([down[:24], jnp.where(row == 7, wrap, edge)], axis=0)
    radial = iota((NODES, SLICE), 1) & 31
    inner = jnp.where(radial > 0, pltpu.roll(field, 1, 1), 0.0)
    outer = jnp.where(radial < 31, pltpu.roll(field, SLICE - 1, 1), 0.0)
    return (up + down) + (inner + outer)


def sweeps_kernel(own_ref, prev_ref, next_ref, got_ref, sig_own_ref, sig_prev_ref, sig_next_ref, back_ref, sig_scr, y_scr, d_scr, sol_scr):
    for first, count, ref in ((0, 2, sig_prev_ref), (2, 4, sig_own_ref), (6, 2, sig_next_ref)):
        for s in range(count):
            turned = ref[s].T
            for block in range(8):
                at = (first + s) * SLICE + block * 32
                sig_scr[:, at : at + 32] = turned[block * 32 : (block + 1) * 32, :]

    def channel_step(channel, _):
        scalar = channel == 3
        vector_numbers = chebyshev_numbers(mass_scale[0])
        scalar_numbers = chebyshev_numbers(mass_scale[3])
        centre, one, two = [
            jnp.where(scalar, b, a).astype(F32) for a, b in zip(vector_numbers, scalar_numbers)
        ]
        mass = jnp.where(scalar, mass_scale[3], mass_scale[0]).astype(F32)
        invert = jnp.where(scalar, 1.0 / scalar_numbers[0], 1.0 / vector_numbers[0]).astype(F32)
        rows = pl.ds(pl.multiple_of(channel * NODES, NODES), NODES)

        def source(s):
            if s < 0:
                return prev_ref[rows, (s + 3) * SLICE : (s + 4) * SLICE]
            if s > 3:
                return next_ref[rows, (s - 4) * SLICE : (s - 3) * SLICE]
            return own_ref[rows, s * SLICE : (s + 1) * SLICE]

        def diag(s):
            return 6.0 + mass * sig_scr[:, (s + 2) * SLICE : (s + 3) * SLICE]

        def held(scr, s):
            return scr[:, (s + 2) * SLICE : (s + 3) * SLICE]

        for s in range(-2, 6):
            here = source(s) * invert
            applied = diag(s) * here - ((source(s - 1) + source(s + 1)) * invert + beside(here))
            rest = source(s) - applied
            y_scr[:, (s + 2) * SLICE : (s + 3) * SLICE] = here + (one * here + two * rest)
        for s in range(-1, 5):
            here = held(y_scr, s)
            applied = diag(s) * here - ((held(y_scr, s - 1) + held(y_scr, s + 1)) + beside(here))
            d_scr[:, (s + 2) * SLICE : (s + 3) * SLICE] = source(s) - applied
        for s in range(0, 4):
            rest = held(d_scr, s)
            here = rest * invert
            applied = diag(s) * here - ((held(d_scr, s - 1) + held(d_scr, s + 1)) * invert + beside(here))
            rest = rest - applied
            value = (held(y_scr, s) + here) + (one * here + two * rest)
            high, low = split(value)
            lanes = slice(s * SLICE, (s + 1) * SLICE)
            sol_scr[rows, lanes] = high
            sol_scr[pl.ds(pl.multiple_of(ROW + channel * NODES, NODES), NODES), lanes] = low
        return 0

    lax.fori_loop(0, 4, channel_step, 0)

    def back_step(step, _):
        part = pl.ds(pl.multiple_of(step * 256, 256), 256)
        label = got_ref[part, LABEL : LABEL + 1].astype(I32)
        hot = one_hot(label == iota((256, BLOCKS), 1) + 1)
        both = dot(hot, sol_scr[...], ((1,), (1,)))
        back_ref[part, :] = both[:, :ROW] + both[:, ROW:]
        return 0

    lax.fori_loop(0, SLOTS // 256, back_step, 0)


def sweeps(own, prev_part, next_part, got, sig_own, sig_prev, sig_next):
    return pl.pallas_call(
        sweeps_kernel,
        out_shape=jax.ShapeDtypeStruct((SLOTS, ROW), F32),
        in_specs=[pl.BlockSpec(memory_space=pltpu.VMEM)] * 7,
        out_specs=pl.BlockSpec(memory_space=pltpu.VMEM),
        scratch_shapes=[
            pltpu.VMEM((NODES, 8 * SLICE), F32),
            pltpu.VMEM((NODES, 8 * SLICE), F32),
            pltpu.VMEM((NODES, 8 * SLICE), F32),
            pltpu.VMEM((2 * ROW, BLOCKS), BF16),
        ],
        compiler_params=pltpu.CompilerParams(vmem_limit_bytes=VMEM_LIMIT),
        name="sweeps",
    )(own, prev_part, next_part, got, sig_own, sig_prev, sig_next)


def lift_kernel(got_ref, slot_ref, res_ref, tan_ref, jac_ref, ends_ref, out_ref, rows_scr, hot_scr, y_scr):
    transposed_rows(got_ref, rows_scr)
    slots = slot_ref[...]

    def hot_step(step, _):
        part = pl.ds(pl.multiple_of(step * 256, 256), 256)
        hot_scr[part, :] = one_hot(slots == iota((256, BLOCKS), 0) + step * 256)
        return 0

    lax.fori_loop(0, SLOTS // 256, hot_step, 0)
    for step in range(BLOCKS // 256):
        lanes = slice(step * 256, (step + 1) * 256)
        both = dot(rows_scr[...], hot_scr[:, lanes], ((1,), (0,)))
        y_scr[:, lanes] = both[:ROW] + both[ROW:]

    def lanes_step(group, _):
        lanes = pl.ds(pl.multiple_of(group * 128, 128), 128)

        def pick(channel, low, quarter):
            parts = [
                jnp.take_along_axis(y_scr[channel * NODES + 8 * k : channel * NODES + 8 * k + 8, lanes], low, axis=0)
                for k in range(4)
            ]
            return jnp.where(
                quarter < 2,
                jnp.where(quarter == 0, parts[0], parts[1]),
                jnp.where(quarter == 2, parts[2], parts[3]),
            )

        for step in range(EDGES // 8):
            edges = slice(step * 8, (step + 1) * 8)
            tail = ends_ref[0, edges, lanes]
            head = ends_ref[1, edges, lanes]
            tail_at = (tail & 7, tail >> 3)
            head_at = (head & 7, head >> 3)
            total = pick(3, *head_at) - pick(3, *tail_at)
            for channel in range(3):
                pair = pick(channel, *head_at) + pick(channel, *tail_at)
                total = total + 0.5 * tan_ref[channel, edges, lanes] * pair
            out_ref[edges, lanes] = jac_ref[edges, lanes] * res_ref[edges, lanes] + total
        return 0

    lax.fori_loop(0, BLOCKS // 128, lanes_step, 0)


def lift(got, slots, residual, tangent, jacobi, ends):
    return pl.pallas_call(
        lift_kernel,
        out_shape=jax.ShapeDtypeStruct((EDGES, BLOCKS), F32),
        in_specs=[pl.BlockSpec(memory_space=pltpu.VMEM)] * 6,
        out_specs=pl.BlockSpec(memory_space=pltpu.VMEM),
        scratch_shapes=[
            pltpu.VMEM((2 * ROW, SLOTS), BF16),
            pltpu.VMEM((SLOTS, BLOCKS), BF16),
            pltpu.VMEM((ROW, BLOCKS), F32),
        ],
        compiler_params=pltpu.CompilerParams(vmem_limit_bytes=VMEM_LIMIT),
        name="lift",
    )(got, slots, residual, tangent, jacobi, ends)


def exchange(rows):
    parts = rows.reshape(DEVICES, CAP, ROW)
    return lax.all_to_all(parts, RING, split_axis=0, concat_axis=0, tiled=True).reshape(SLOTS, ROW)


def per_device(residual, tangent, jacobi, ends, target, node_block, sigma):
    slabs = range(DEVICES)
    forward = [(place(s), place((s + 1) % DEVICES)) for s in slabs]
    backward = [(place((s + 1) % DEVICES), place(s)) for s in slabs]
    sig_own = lax.ppermute(sigma, RING, [(s, place(s)) for s in slabs])
    sig_prev = lax.ppermute(sigma[2:], RING, [(s, place((s + 1) % DEVICES)) for s in slabs])
    sig_next = lax.ppermute(sigma[:2], RING, [((s + 1) % DEVICES, place(s)) for s in slabs])
    send, slots = edge_terms(
        residual, tangent, ends, target.reshape(1, BLOCKS), node_block.reshape(1, BLOCKS)
    )
    got = exchange(send)
    own, to_prev, to_next = block_sums(got)
    prev_part = lax.ppermute(to_next, RING, forward)
    next_part = lax.ppermute(to_prev, RING, backward)
    back = sweeps(own, prev_part, next_part, got, sig_own, sig_prev, sig_next)
    mine = exchange(back)
    return lift(mine, slots, residual, tangent, jacobi, ends)


def solution(mesh):
    in_specs = (
        P(None, RING),
        P(None, None, RING),
        P(None, RING),
        P(None, None, RING),
        P(RING, None),
        P(RING),
        P(RING, None, None),
    )
    return jax.shard_map(
        per_device, mesh=mesh, in_specs=in_specs, out_specs=P(None, RING), check_vma=False
    )
```

```python
import jax
import jax.numpy as jnp
from jax import lax
from jax.experimental import pallas as pl
from jax.experimental.pallas import tpu as pltpu
from jax.sharding import PartitionSpec as P

F32 = jnp.float32
BF16 = jnp.bfloat16
I32 = jnp.int32

EDGES = 64
NODES = 32
ROW = 4 * NODES
BLOCKS = 1024
CAP = 16
DEVICES = 128
SLOTS = DEVICES * CAP
SLICE = 256
HALO = 3 * SLICE
LABEL = 3 * NODES
RING = ("edge", "node")
VMEM_LIMIT = 24 * 1024 * 1024
FIRST_LIMIT = 60 * 1024 * 1024
MESSAGE = ROW + 24

mass_scale = (1.0, 1.0, 1.0, 0.5)


def chebyshev_numbers(scale):
    upper = 12.0 + 8.0 * scale
    lower = upper / 8.0
    centre = (upper + lower) / 2.0
    radius = (upper - lower) / 2.0
    ratio = centre / radius
    first = 1.0 / ratio
    second = 1.0 / (2.0 * ratio - first)
    return (centre, second * first, 2.0 * second / radius)


def place(slab):
    return slab ^ (24 * ((slab >> 5) & 1)) ^ (6 * ((slab >> 3) & 1))


def split(value):
    high = value.astype(BF16)
    return high, (value - high.astype(F32)).astype(BF16)


def one_hot(mask):
    return jnp.where(mask, 1.0, 0.0).astype(BF16)


def iota(shape, dim):
    return lax.broadcasted_iota(I32, shape, dim)


def dot(left, right, dims):
    return lax.dot_general(left, right, (dims, ((), ())), preferred_element_type=F32)


def terms_kernel(
    target_hbm, block_hbm, res_hbm, tan_hbm, ends_hbm, send_hbm, slot_hbm,
    target_scr, block_scr, res_scr, tan_scr, ends_scr, term_scr, acc_scr, row_scr, send_scr, slot_ref, label_scr, place_scr,
    place_sem, list_sem, in_sem, out_sem,
):
    groups = BLOCKS // 128

    def fetch(group):
        lanes = pl.ds(group * 128, 128)
        return [
            pltpu.make_async_copy(hbm.at[..., lanes], scr.at[..., lanes], in_sem.at[i, group])
            for i, (hbm, scr) in enumerate(((ends_hbm, ends_scr), (res_hbm, res_scr), (tan_hbm, tan_scr)))
        ]

    lists = [
        pltpu.make_async_copy(target_hbm, target_scr, list_sem.at[0]),
        pltpu.make_async_copy(block_hbm, block_scr, list_sem.at[1]),
    ]
    for copy in lists:
        copy.start()
    for group in range(groups):
        for copy in fetch(group):
            copy.start()
    send_scr[...] = jnp.zeros((SLOTS, ROW), F32)
    node = iota((NODES, 128), 0)

    def turn(group):
        lanes = pl.ds(pl.multiple_of(group * 128, 128), 128)
        acc_scr[group, LABEL : LABEL + 1, :] = label_scr[:, lanes]
        row_scr[lanes, :] = acc_scr[group].T

    def post(group, step):
        for inner in range(16):
            block = group * 128 + step * 16 + inner
            send_scr[pl.ds(place_scr[0, block], 1), :] = row_scr[pl.ds(block, 1), :]

    def edge_step(step, lanes, sums):
        sums = list(sums)
        for inner in range(8):
            row = slice(inner, inner + 1)
            head = ends_scr[1, step, row, lanes] == node
            tail = ends_scr[0, step, row, lanes] == node
            either = head | tail
            value = res_scr[step, row, lanes]
            for channel in range(3):
                term = term_scr[channel, step, row, :]
                sums[channel] = sums[channel] + jnp.where(either, term, 0.0)
            sums[3] = sums[3] + jnp.where(head, value, jnp.where(tail, -value, 0.0))
        return tuple(sums)

    def lanes_step(group, turned, posted):
        lanes = pl.ds(pl.multiple_of(group * 128, 128), 128)
        for i, (hbm, scr) in enumerate(((ends_hbm, ends_scr), (res_hbm, res_scr), (tan_hbm, tan_scr))):
            pltpu.make_async_copy(hbm.at[..., lanes], scr.at[..., lanes], in_sem.at[i, group]).wait()
        term_scr[...] = 0.5 * tan_scr[:, :, :, lanes] * res_scr[:, :, lanes][None]
        if turned:
            turn(group - 1)
        if posted:
            post(group - 2, 0)
        sums = edge_step(0, lanes, (jnp.zeros((NODES, 128), F32),) * 4)

        def tile_step(step, sums):
            if posted:
                post(group - 2, step)
            return edge_step(step, lanes, sums)

        sums = lax.fori_loop(1, EDGES // 8, tile_step, sums)
        for channel in range(3):
            acc_scr[group, channel * NODES : (channel + 1) * NODES, :] = sums[channel]
        acc_scr[group, LABEL:, :] = sums[3]

    lanes_step(0, False, False)
    for copy in lists:
        copy.wait()

    holder = place(target_scr[...])
    device = iota((DEVICES, 128), 0)
    before = one_hot(iota((128, 128), 0) < iota((128, 128), 1))
    seen = jnp.zeros((DEVICES, 1), F32)
    for group in range(groups):
        lanes = slice(group * 128, (group + 1) * 128)
        same = holder[:, lanes] == device
        hot = jnp.where(same, 1.0, 0.0)
        count = dot(hot.astype(BF16), before, ((1,), (0,))) + seen
        rank = jnp.sum(jnp.where(same, count, 0.0), axis=0, keepdims=True)
        slot_ref[:, lanes] = holder[:, lanes] * CAP + rank.astype(I32)
        seen = seen + jnp.sum(hot, axis=1, keepdims=True)
    to_scalar = pltpu.make_async_copy(slot_ref, place_scr, place_sem.at[0])
    to_scalar.start()
    to_lift = pltpu.make_async_copy(slot_ref, slot_hbm, place_sem.at[1])
    to_lift.start()

    number = block_scr[...]
    label = (number & ~255) + (number & 7) * 32 + ((number >> 3) & 31)
    label = (label + 1).astype(F32)
    label_scr[...] = label

    lanes_step(1, True, False)
    to_scalar.wait()

    def group_step(group, _):
        lanes_step(group, True, True)
        return 0

    lax.fori_loop(2, groups, group_step, 0)
    turn(groups - 1)
    for group in (groups - 2, groups - 1):
        for step in range(8):
            post(group, step)
    parts = 8
    out = []
    for part in range(parts):
        rows = pl.ds(part * (SLOTS // parts), SLOTS // parts)
        out.append(pltpu.make_async_copy(send_scr.at[rows, :], send_hbm.at[rows, :], out_sem.at[part]))
    for copy in out:
        copy.start()
    for copy in out:
        copy.wait()
    to_lift.wait()


def edge_terms(residual, tangent, ends, target, node_block):
    tiles = EDGES // 8
    hbm = pl.BlockSpec(memory_space=pltpu.HBM)
    return pl.pallas_call(
        terms_kernel,
        out_shape=(
            jax.ShapeDtypeStruct((SLOTS, ROW), F32),
            jax.ShapeDtypeStruct((1, BLOCKS), I32),
        ),
        in_specs=[hbm] * 5,
        out_specs=[hbm, hbm],
        scratch_shapes=[
            pltpu.VMEM((1, BLOCKS), I32),
            pltpu.VMEM((1, BLOCKS), I32),
            pltpu.VMEM((tiles, 8, BLOCKS), F32),
            pltpu.VMEM((3, tiles, 8, BLOCKS), F32),
            pltpu.VMEM((2, tiles, 8, BLOCKS), I32),
            pltpu.VMEM((3, tiles, 8, 128), F32),
            pltpu.VMEM((BLOCKS // 128, ROW, 128), F32),
            pltpu.VMEM((BLOCKS, ROW), F32),
            pltpu.VMEM((SLOTS, ROW), F32),
            pltpu.VMEM((1, BLOCKS), I32),
            pltpu.VMEM((1, BLOCKS), F32),
            pltpu.SMEM((1, BLOCKS), I32),
            pltpu.SemaphoreType.DMA((2,)),
            pltpu.SemaphoreType.DMA((2,)),
            pltpu.SemaphoreType.DMA((3, BLOCKS // 128)),
            pltpu.SemaphoreType.DMA((8,)),
        ],
        compiler_params=pltpu.CompilerParams(vmem_limit_bytes=FIRST_LIMIT),
        cost_estimate=pl.CostEstimate(flops=50_000_000, bytes_accessed=20_000_000, transcendentals=0),
        name="edge_terms",
    )(
        target,
        node_block,
        residual.reshape(tiles, 8, BLOCKS),
        tangent.reshape(3, tiles, 8, BLOCKS),
        ends.reshape(2, tiles, 8, BLOCKS),
    )


def sums_kernel(got_ref, sigma_ref, own_ref, before_ref, after_ref, from_ref, sig_ref, rows_scr, hot_scr):
    for step in range(SLOTS // 128):
        part = slice(step * 128, (step + 1) * 128)
        turned = got_ref[part, :].T
        high, low = split(turned)
        rows_scr[0:ROW, part] = high
        rows_scr[ROW:, part] = low
        label = turned[LABEL : LABEL + 1, :].astype(I32)
        from_ref[step : step + 1, :] = jnp.maximum(label - 1, 0)
        column = got_ref[part, LABEL : LABEL + 1].astype(I32)
        hot_scr[part, :] = one_hot(column == iota((128, BLOCKS), 1) + 1)

    for step in range(BLOCKS // 256):
        lanes = slice(step * 256, (step + 1) * 256)
        both = dot(rows_scr[...], hot_scr[:, lanes], ((1,), (0,)))
        sums = both[:ROW] + both[ROW:]
        scalar = sums[LABEL:]
        first = iota((NODES, 256), 0) == 0
        rest = -jnp.sum(jnp.where(first, 0.0, scalar), axis=0, keepdims=True)
        own_ref[0:LABEL, lanes] = sums[:LABEL]
        own_ref[LABEL:, lanes] = jnp.where(first, rest, scalar)
    before_ref[0:ROW, :] = own_ref[:, 0:HALO]
    after_ref[0:ROW, :] = own_ref[:, BLOCKS - HALO :]

    for s in range(4):
        turned = sigma_ref[s].T
        for block in range(8):
            at = s * SLICE + block * 32
            sig_ref[:, at : at + 32] = turned[block * 32 : (block + 1) * 32, :]
    for ref, first in ((before_ref, 0), (after_ref, 2)):
        ref[ROW:, 0 : 2 * SLICE] = sig_ref[0:24, first * SLICE : (first + 2) * SLICE]
        for s in range(2):
            ref[ROW + 8 * s : ROW + 8 * s + 8, 2 * SLICE :] = sig_ref[24:, (first + s) * SLICE : (first + s + 1) * SLICE]
        ref[ROW + 16 :, 2 * SLICE :] = jnp.zeros((8, SLICE), F32)


def block_sums(got, sigma):
    vmem = pl.BlockSpec(memory_space=pltpu.VMEM)
    return pl.pallas_call(
        sums_kernel,
        out_shape=(
            jax.ShapeDtypeStruct((ROW, BLOCKS), F32),
            jax.ShapeDtypeStruct((MESSAGE, HALO), F32),
            jax.ShapeDtypeStruct((MESSAGE, HALO), F32),
            jax.ShapeDtypeStruct((SLOTS // 128, 128), I32),
            jax.ShapeDtypeStruct((NODES, BLOCKS), F32),
        ),
        in_specs=[vmem] * 2,
        out_specs=[vmem] * 5,
        scratch_shapes=[
            pltpu.VMEM((2 * ROW, SLOTS), BF16),
            pltpu.VMEM((SLOTS, BLOCKS), BF16),
        ],
        compiler_params=pltpu.CompilerParams(vmem_limit_bytes=VMEM_LIMIT),
        cost_estimate=pl.CostEstimate(flops=1_100_000_000, bytes_accessed=5_000_000, transcendentals=0),
        name="block_sums",
    )(got, sigma)


def sweeps_kernel(
    own_ref, prev_ref, next_ref, sig_ref, from_ref, back_ref,
    diag_scr, d_scr, y_scr, p_scr, keep_scr, sol_scr, row_scr,
):
    tiles = NODES // 8
    lane = iota((8, 128), 1)
    row = iota((8, 128), 0)
    low, high = (lane & 31) > 0, (lane & 31) < 31
    bottom, top = row == 0, row == 7

    def put(scr, s, half, tile, value):
        scr[s + 3, half, tile * 8 : tile * 8 + 8, :] = value

    def get(scr, s, half, tile):
        return scr[s + 3, half, tile * 8 : tile * 8 + 8, :]

    def beside(scr, s):
        here = [[get(scr, s, half, tile) for tile in range(tiles)] for half in range(2)]
        up = [[pltpu.roll(value, 1, 0) for value in part] for part in here]
        down = [[pltpu.roll(value, 7, 0) for value in part] for part in here]
        first = [pltpu.roll(part[-1], 32, 1) for part in up]
        last = [pltpu.roll(part[0], 96, 1) for part in down]
        first = [jnp.where(lane < 32, 0.0, first[0]), jnp.where(lane < 32, first[0], first[1])]
        last = [jnp.where(lane < 96, last[0], last[1]), jnp.where(lane < 96, last[1], 0.0)]
        sums = []
        for half in range(2):
            sums.append([])
            for tile in range(tiles):
                below = up[half][tile - 1] if tile else first[half]
                above = down[half][tile + 1] if tile < tiles - 1 else last[half]
                axial = jnp.where(bottom, below, up[half][tile]) + jnp.where(top, above, down[half][tile])
                value = here[half][tile]
                inner = jnp.where(low, pltpu.roll(value, 1, 1), 0.0)
                outer = jnp.where(high, pltpu.roll(value, 127, 1), 0.0)
                sums[half].append((axial + inner) + outer)
        return sums

    def apply(scr, s, kind):
        near = beside(scr, s)
        for half in range(2):
            for tile in range(tiles):
                here = get(scr, s, half, tile)
                beyond = get(scr, s - 1, half, tile) + get(scr, s + 1, half, tile)
                diag = diag_scr[kind, s + 2, half, tile * 8 : tile * 8 + 8, :]
                yield half, tile, here, diag * here - (beyond + near[half][tile])

    def keep_diag(s, half, rows, sig):
        for i, mass in enumerate((mass_scale[0], mass_scale[3])):
            diag_scr[i, s + 2, half, rows, :] = 6.0 + mass * sig

    every, upper, lower = slice(0, NODES), slice(0, 24), slice(24, NODES)
    for half in range(2):
        for s in range(4):
            keep_diag(s, half, every, sig_ref[:, s * SLICE + half * 128 : s * SLICE + half * 128 + 128])
        for ref, first in ((prev_ref, -2), (next_ref, 4)):
            for s in range(2):
                at = s * SLICE + half * 128
                keep_diag(first + s, half, upper, ref[ROW:, at : at + 128])
                at = 2 * SLICE + half * 128
                keep_diag(first + s, half, lower, ref[ROW + 8 * s : ROW + 8 * s + 8, at : at + 128])

    def channel_step(channel, _):
        scalar = channel == 3
        vector_numbers = chebyshev_numbers(mass_scale[0])
        scalar_numbers = chebyshev_numbers(mass_scale[3])
        _, one, two = [
            jnp.where(scalar, b, a).astype(F32) for a, b in zip(vector_numbers, scalar_numbers)
        ]
        invert = jnp.where(scalar, 1.0 / scalar_numbers[0], 1.0 / vector_numbers[0]).astype(F32)
        kind = jnp.where(scalar, 1, 0)
        base = channel * NODES

        def rows(tile):
            return pl.ds(pl.multiple_of(base + tile * 8, 8), 8)

        def source(s, half, tile):
            if s < 0:
                ref, s = prev_ref, s + 3
            elif s > 3:
                ref, s = next_ref, s - 4
            else:
                ref = own_ref
            return ref[rows(tile), s * SLICE + half * 128 : s * SLICE + half * 128 + 128]

        for s in range(-3, 7):
            for half in range(2):
                for tile in range(tiles):
                    put(d_scr, s, half, tile, source(s, half, tile) * invert)
        for s in range(-2, 6):
            for half, tile, here, applied in apply(d_scr, s, kind):
                rest = source(s, half, tile) - applied
                put(y_scr, s, half, tile, here + (one * here + two * rest))
        for s in range(-1, 5):
            for half, tile, here, applied in apply(y_scr, s, kind):
                rest = source(s, half, tile) - applied
                put(p_scr, s, half, tile, rest * invert)
                if 0 <= s < 4:
                    keep_scr[s, half, tile * 8 : tile * 8 + 8, :] = rest
        for s in range(4):
            for half, tile, here, applied in apply(p_scr, s, kind):
                rest = keep_scr[s, half, tile * 8 : tile * 8 + 8, :] - applied
                at = s * SLICE + half * 128
                value = (get(y_scr, s, half, tile) + here) + (one * here + two * rest)
                sol_scr[rows(tile), at : at + 128] = value
        return 0

    lax.fori_loop(0, 4, channel_step, 0)
    for group in range(BLOCKS // 128):
        part = slice(group * 128, (group + 1) * 128)
        row_scr[part, :] = sol_scr[:, part].T
    for slot in range(SLOTS):
        back_ref[slot : slot + 1, :] = row_scr[pl.ds(from_ref[slot // 128, slot % 128], 1), :]


def sweeps(own, prev_part, next_part, sig, labels):
    vmem = pl.BlockSpec(memory_space=pltpu.VMEM)
    field = pltpu.VMEM((10, 2, NODES, 128), F32)
    return pl.pallas_call(
        sweeps_kernel,
        out_shape=jax.ShapeDtypeStruct((SLOTS, ROW), F32),
        in_specs=[vmem, vmem, vmem, vmem, pl.BlockSpec(memory_space=pltpu.SMEM)],
        out_specs=vmem,
        scratch_shapes=[
            pltpu.VMEM((2, 8, 2, NODES, 128), F32),
            field,
            field,
            field,
            pltpu.VMEM((4, 2, NODES, 128), F32),
            pltpu.VMEM((ROW, BLOCKS), F32),
            pltpu.VMEM((BLOCKS, ROW), F32),
        ],
        compiler_params=pltpu.CompilerParams(vmem_limit_bytes=VMEM_LIMIT),
        name="sweeps",
    )(own, prev_part, next_part, sig, labels)


def lift_kernel(got_ref, slot_ref, res_ref, tan_ref, jac_ref, ends_ref, out_hbm, row_scr, y_scr, out_ref, out_sem):
    def take(group, step):
        for inner in range(16):
            block = group * 128 + step * 16 + inner
            row_scr[block : block + 1, :] = got_ref[pl.ds(slot_ref[0, block], 1), :]

    def turn(group):
        y_scr[group] = row_scr[group * 128 : (group + 1) * 128, :].T

    groups = BLOCKS // 128
    for step in range(8):
        take(0, step)
    turn(0)
    for group in range(groups):
        lanes = slice(group * 128, (group + 1) * 128)

        def pick(channel, low, quarter):
            parts = [
                jnp.take_along_axis(y_scr[group, channel * NODES + 8 * k : channel * NODES + 8 * k + 8, :], low, axis=0)
                for k in range(4)
            ]
            return jnp.where(
                quarter < 2,
                jnp.where(quarter == 0, parts[0], parts[1]),
                jnp.where(quarter == 2, parts[2], parts[3]),
            )

        for step in range(EDGES // 8):
            if group + 1 < groups:
                take(group + 1, step)
            edges = slice(step * 8, (step + 1) * 8)
            tail = ends_ref[0, edges, lanes]
            head = ends_ref[1, edges, lanes]
            tail_at = (tail & 7, tail >> 3)
            head_at = (head & 7, head >> 3)
            total = pick(3, *head_at) - pick(3, *tail_at)
            for channel in range(3):
                pair = pick(channel, *head_at) + pick(channel, *tail_at)
                total = total + 0.5 * tan_ref[channel, edges, lanes] * pair
            out_ref[edges, lanes] = jac_ref[edges, lanes] * res_ref[edges, lanes] + total
        if group + 1 < groups:
            turn(group + 1)
        pltpu.make_async_copy(out_ref.at[:, lanes], out_hbm.at[:, lanes], out_sem.at[group]).start()
    for group in range(groups):
        lanes = slice(group * 128, (group + 1) * 128)
        pltpu.make_async_copy(out_ref.at[:, lanes], out_hbm.at[:, lanes], out_sem.at[group]).wait()


def lift(got, slots, residual, tangent, jacobi, ends):
    vmem = pl.BlockSpec(memory_space=pltpu.VMEM)
    return pl.pallas_call(
        lift_kernel,
        out_shape=jax.ShapeDtypeStruct((EDGES, BLOCKS), F32),
        in_specs=[vmem, pl.BlockSpec(memory_space=pltpu.SMEM), vmem, vmem, vmem, vmem],
        out_specs=pl.BlockSpec(memory_space=pltpu.HBM),
        scratch_shapes=[
            pltpu.VMEM((BLOCKS, ROW), F32),
            pltpu.VMEM((BLOCKS // 128, ROW, 128), F32),
            pltpu.VMEM((EDGES, BLOCKS), F32),
            pltpu.SemaphoreType.DMA((BLOCKS // 128,)),
        ],
        compiler_params=pltpu.CompilerParams(vmem_limit_bytes=VMEM_LIMIT),
        name="lift",
    )(got, slots, residual, tangent, jacobi, ends)


def exchange(rows):
    parts = rows.reshape(DEVICES, CAP, ROW)
    return lax.all_to_all(parts, RING, split_axis=0, concat_axis=0, tiled=True).reshape(SLOTS, ROW)


def per_device(residual, tangent, jacobi, ends, target, node_block, sigma):
    slabs = range(DEVICES)
    forward = [(place(s), place((s + 1) % DEVICES)) for s in slabs]
    backward = [(place((s + 1) % DEVICES), place(s)) for s in slabs]
    sig_own = lax.ppermute(sigma, RING, [(s, place(s)) for s in slabs])
    send, slots = edge_terms(
        residual, tangent, ends, target.reshape(1, BLOCKS), node_block.reshape(1, BLOCKS)
    )
    send, sig_own = lax.optimization_barrier((send, sig_own))
    got = exchange(send)
    own, to_prev, to_next, labels, sig = block_sums(got, sig_own)
    prev_part = lax.ppermute(to_next, RING, forward)
    next_part = lax.ppermute(to_prev, RING, backward)
    back = sweeps(own, prev_part, next_part, sig, labels)
    mine = exchange(back)
    return lift(mine, slots, residual, tangent, jacobi, ends)


def solution(mesh):
    in_specs = (
        P(None, RING),
        P(None, None, RING),
        P(None, RING),
        P(None, None, RING),
        P(RING, None),
        P(RING),
        P(RING, None, None),
    )
    return jax.shard_map(
        per_device, mesh=mesh, in_specs=in_specs, out_specs=P(None, RING), check_vma=False
    )
```

```python
import jax
import jax.numpy as jnp
from jax import lax
from jax.experimental import pallas as pl
from jax.experimental.pallas import tpu as pltpu
from jax.sharding import PartitionSpec as P

F32 = jnp.float32
BF16 = jnp.bfloat16
I32 = jnp.int32

EDGES = 64
NODES = 32
ROW = 4 * NODES
BLOCKS = 1024
CAP = 16
DEVICES = 128
SLOTS = DEVICES * CAP
SLICE = 256
HALO = 3 * SLICE
LABEL = 3 * NODES
RING = ("edge", "node")
VMEM_LIMIT = 24 * 1024 * 1024
FIRST_LIMIT = 60 * 1024 * 1024
MESSAGE = ROW + 24

mass_scale = (1.0, 1.0, 1.0, 0.5)


def chebyshev_numbers(scale):
    upper = 12.0 + 8.0 * scale
    lower = upper / 8.0
    centre = (upper + lower) / 2.0
    radius = (upper - lower) / 2.0
    ratio = centre / radius
    first = 1.0 / ratio
    second = 1.0 / (2.0 * ratio - first)
    return (centre, second * first, 2.0 * second / radius)


def place(slab):
    return slab ^ (24 * ((slab >> 5) & 1)) ^ (6 * ((slab >> 3) & 1))


def odd_slab():
    return lax.axis_index("node") & 1


def split(value):
    high = value.astype(BF16)
    return high, (value - high.astype(F32)).astype(BF16)


def one_hot(mask):
    return jnp.where(mask, 1.0, 0.0).astype(BF16)


def iota(shape, dim):
    return lax.broadcasted_iota(I32, shape, dim)


def dot(left, right, dims):
    return lax.dot_general(left, right, (dims, ((), ())), preferred_element_type=F32)


def terms_kernel(
    target_hbm, block_hbm, res_hbm, tan_hbm, ends_hbm, send_hbm, slot_hbm,
    target_scr, block_scr, res_scr, tan_scr, ends_scr, term_scr, acc_scr, row_scr, send_scr, slot_ref, label_scr, place_scr,
    place_sem, list_sem, in_sem, out_sem,
):
    groups = BLOCKS // 128

    chunks = ((0, 128), (128, 128), (256, BLOCKS - 256))

    def fetch(chunk):
        lanes = pl.ds(*chunks[chunk])
        return [
            pltpu.make_async_copy(hbm.at[..., lanes], scr.at[..., lanes], in_sem.at[i, chunk])
            for i, (hbm, scr) in enumerate(((ends_hbm, ends_scr), (res_hbm, res_scr), (tan_hbm, tan_scr)))
        ]

    lists = [
        pltpu.make_async_copy(target_hbm, target_scr, list_sem.at[0]),
        pltpu.make_async_copy(block_hbm, block_scr, list_sem.at[1]),
    ]
    fetched = [fetch(chunk) for chunk in range(3)]
    for copy in fetched[0] + lists + fetched[1] + fetched[2]:
        copy.start()
    send_scr[...] = jnp.zeros((SLOTS, ROW), F32)
    node = iota((NODES, 128), 0)

    def turn(group):
        lanes = pl.ds(pl.multiple_of(group * 128, 128), 128)
        acc_scr[group, LABEL : LABEL + 1, :] = label_scr[:, lanes]
        row_scr[lanes, :] = acc_scr[group].T

    def post(group, step):
        for inner in range(16):
            block = group * 128 + step * 16 + inner
            send_scr[pl.ds(place_scr[0, block], 1), :] = row_scr[pl.ds(block, 1), :]

    def edge_step(step, lanes, sums):
        sums = list(sums)
        for inner in range(8):
            row = slice(inner, inner + 1)
            head = ends_scr[1, step, row, lanes] == node
            tail = ends_scr[0, step, row, lanes] == node
            either = head | tail
            value = res_scr[step, row, lanes]
            for channel in range(3):
                term = term_scr[channel, step, row, :]
                sums[channel] = sums[channel] + jnp.where(either, term, 0.0)
            sums[3] = sums[3] + jnp.where(head, value, jnp.where(tail, -value, 0.0))
        return tuple(sums)

    def lanes_step(group, turned, posted):
        lanes = pl.ds(pl.multiple_of(group * 128, 128), 128)
        term_scr[...] = 0.5 * tan_scr[:, :, :, lanes] * res_scr[:, :, lanes][None]
        if turned:
            turn(group - 1)
        if posted:
            post(group - 2, 0)
        sums = edge_step(0, lanes, (jnp.zeros((NODES, 128), F32),) * 4)

        def tile_step(step, sums):
            if posted:
                post(group - 2, step)
            return edge_step(step, lanes, sums)

        sums = lax.fori_loop(1, EDGES // 8, tile_step, sums)
        for channel in range(3):
            acc_scr[group, channel * NODES : (channel + 1) * NODES, :] = sums[channel]
        acc_scr[group, LABEL:, :] = sums[3]

    for copy in fetched[0]:
        copy.wait()
    lanes_step(0, False, False)
    for copy in lists:
        copy.wait()

    holder = place(target_scr[...])
    device = iota((DEVICES, 128), 0)
    before = one_hot(iota((128, 128), 0) < iota((128, 128), 1))
    seen = jnp.zeros((DEVICES, 1), F32)
    for group in range(groups):
        lanes = slice(group * 128, (group + 1) * 128)
        same = holder[:, lanes] == device
        hot = jnp.where(same, 1.0, 0.0)
        count = dot(hot.astype(BF16), before, ((1,), (0,))) + seen
        rank = jnp.sum(jnp.where(same, count, 0.0), axis=0, keepdims=True)
        slot_ref[:, lanes] = holder[:, lanes] * CAP + rank.astype(I32)
        seen = seen + jnp.sum(hot, axis=1, keepdims=True)
    to_scalar = pltpu.make_async_copy(slot_ref, place_scr, place_sem.at[0])
    to_scalar.start()
    to_lift = pltpu.make_async_copy(slot_ref, slot_hbm, place_sem.at[1])
    to_lift.start()

    number = block_scr[...]
    label = (number & ~255) + (number & 7) * 32 + ((number >> 3) & 31)
    label = (label + 1).astype(F32)
    label_scr[...] = label

    for copy in fetched[1]:
        copy.wait()
    lanes_step(1, True, False)
    for copy in fetched[2]:
        copy.wait()
    to_scalar.wait()

    def group_step(group, _):
        lanes_step(group, True, True)
        return 0

    lax.fori_loop(2, groups, group_step, 0)
    turn(groups - 1)
    for group in (groups - 2, groups - 1):
        for step in range(8):
            post(group, step)
    parts = 8
    out = []
    for part in range(parts):
        rows = pl.ds(part * (SLOTS // parts), SLOTS // parts)
        out.append(pltpu.make_async_copy(send_scr.at[rows, :], send_hbm.at[rows, :], out_sem.at[part]))
    for copy in out:
        copy.start()
    for copy in out:
        copy.wait()
    to_lift.wait()


def edge_terms(residual, tangent, ends, target, node_block):
    tiles = EDGES // 8
    hbm = pl.BlockSpec(memory_space=pltpu.HBM)
    return pl.pallas_call(
        terms_kernel,
        out_shape=(
            jax.ShapeDtypeStruct((SLOTS, ROW), F32),
            jax.ShapeDtypeStruct((1, BLOCKS), I32),
        ),
        in_specs=[hbm] * 5,
        out_specs=[hbm, hbm],
        scratch_shapes=[
            pltpu.VMEM((1, BLOCKS), I32),
            pltpu.VMEM((1, BLOCKS), I32),
            pltpu.VMEM((tiles, 8, BLOCKS), F32),
            pltpu.VMEM((3, tiles, 8, BLOCKS), F32),
            pltpu.VMEM((2, tiles, 8, BLOCKS), I32),
            pltpu.VMEM((3, tiles, 8, 128), F32),
            pltpu.VMEM((BLOCKS // 128, ROW, 128), F32),
            pltpu.VMEM((BLOCKS, ROW), F32),
            pltpu.VMEM((SLOTS, ROW), F32),
            pltpu.VMEM((1, BLOCKS), I32),
            pltpu.VMEM((1, BLOCKS), F32),
            pltpu.SMEM((1, BLOCKS), I32),
            pltpu.SemaphoreType.DMA((2,)),
            pltpu.SemaphoreType.DMA((2,)),
            pltpu.SemaphoreType.DMA((3, 3)),
            pltpu.SemaphoreType.DMA((8,)),
        ],
        compiler_params=pltpu.CompilerParams(vmem_limit_bytes=FIRST_LIMIT),
        cost_estimate=pl.CostEstimate(flops=50_000_000, bytes_accessed=20_000_000, transcendentals=0),
        name="edge_terms",
    )(
        target,
        node_block,
        residual.reshape(tiles, 8, BLOCKS),
        tangent.reshape(3, tiles, 8, BLOCKS),
        ends.reshape(2, tiles, 8, BLOCKS),
    )


def sums_kernel(got_ref, sigma_ref, own_ref, far_ref, near_ref, from_ref, sig_ref, rows_scr, hot_scr):
    for step in range(SLOTS // 128):
        part = slice(step * 128, (step + 1) * 128)
        turned = got_ref[part, :].T
        high, low = split(turned)
        rows_scr[0:ROW, part] = high
        rows_scr[ROW:, part] = low
        label = turned[LABEL : LABEL + 1, :].astype(I32)
        from_ref[step : step + 1, :] = jnp.maximum(label - 1, 0)
        column = got_ref[part, LABEL : LABEL + 1].astype(I32)
        hot_scr[part, :] = one_hot(column == iota((128, BLOCKS), 1) + 1)

    for step in range(BLOCKS // 256):
        lanes = slice(step * 256, (step + 1) * 256)
        both = dot(rows_scr[...], hot_scr[:, lanes], ((1,), (0,)))
        sums = both[:ROW] + both[ROW:]
        scalar = sums[LABEL:]
        first = iota((NODES, 256), 0) == 0
        rest = -jnp.sum(jnp.where(first, 0.0, scalar), axis=0, keepdims=True)
        own_ref[0:LABEL, lanes] = sums[:LABEL]
        own_ref[LABEL:, lanes] = jnp.where(first, rest, scalar)
    for s in range(4):
        turned = sigma_ref[s].T
        for block in range(8):
            at = s * SLICE + block * 32
            sig_ref[:, at : at + 32] = turned[block * 32 : (block + 1) * 32, :]
    odd = odd_slab()
    for ref, after in ((far_ref, odd), (near_ref, 1 - odd)):
        ref[0:ROW, :] = own_ref[:, pl.ds(pl.multiple_of(after * SLICE, SLICE), HALO)]
        lanes = pl.ds(pl.multiple_of(after * (2 * SLICE), 2 * SLICE), 2 * SLICE)
        ref[ROW:, 0 : 2 * SLICE] = sig_ref[0:24, lanes]
        for s in range(2):
            lanes = pl.ds(pl.multiple_of((2 * after + s) * SLICE, SLICE), SLICE)
            ref[ROW + 8 * s : ROW + 8 * s + 8, 2 * SLICE :] = sig_ref[24:, lanes]
        ref[ROW + 16 :, 2 * SLICE :] = jnp.zeros((8, SLICE), F32)


def block_sums(got, sigma):
    vmem = pl.BlockSpec(memory_space=pltpu.VMEM)
    return pl.pallas_call(
        sums_kernel,
        out_shape=(
            jax.ShapeDtypeStruct((ROW, BLOCKS), F32),
            jax.ShapeDtypeStruct((MESSAGE, HALO), F32),
            jax.ShapeDtypeStruct((MESSAGE, HALO), F32),
            jax.ShapeDtypeStruct((SLOTS // 128, 128), I32),
            jax.ShapeDtypeStruct((NODES, BLOCKS), F32),
        ),
        in_specs=[vmem] * 2,
        out_specs=[vmem] * 5,
        scratch_shapes=[
            pltpu.VMEM((2 * ROW, SLOTS), BF16),
            pltpu.VMEM((SLOTS, BLOCKS), BF16),
        ],
        compiler_params=pltpu.CompilerParams(vmem_limit_bytes=VMEM_LIMIT),
        cost_estimate=pl.CostEstimate(flops=1_100_000_000, bytes_accessed=5_000_000, transcendentals=0),
        name="block_sums",
    )(got, sigma)


def sweeps_kernel(
    own_ref, far_ref, near_ref, sig_ref, from_ref, back_ref,
    diag_scr, d_scr, y_scr, p_scr, keep_scr, sol_scr, row_scr, place_scr, place_sem,
):
    to_scalar = pltpu.make_async_copy(from_ref, place_scr, place_sem)
    to_scalar.start()
    odd = odd_slab() == 1

    def halo(behind, index):
        far, near = far_ref[index], near_ref[index]
        return jnp.where(odd, near, far) if behind else jnp.where(odd, far, near)

    tiles = NODES // 8
    lane = iota((8, 128), 1)
    row = iota((8, 128), 0)
    low, high = (lane & 31) > 0, (lane & 31) < 31
    bottom, top = row == 0, row == 7

    def put(scr, s, half, tile, value):
        scr[s + 3, half, tile * 8 : tile * 8 + 8, :] = value

    def get(scr, s, half, tile):
        return scr[s + 3, half, tile * 8 : tile * 8 + 8, :]

    def beside(scr, s):
        here = [[get(scr, s, half, tile) for tile in range(tiles)] for half in range(2)]
        up = [[pltpu.roll(value, 1, 0) for value in part] for part in here]
        down = [[pltpu.roll(value, 7, 0) for value in part] for part in here]
        first = [pltpu.roll(part[-1], 32, 1) for part in up]
        last = [pltpu.roll(part[0], 96, 1) for part in down]
        first = [jnp.where(lane < 32, 0.0, first[0]), jnp.where(lane < 32, first[0], first[1])]
        last = [jnp.where(lane < 96, last[0], last[1]), jnp.where(lane < 96, last[1], 0.0)]
        sums = []
        for half in range(2):
            sums.append([])
            for tile in range(tiles):
                below = up[half][tile - 1] if tile else first[half]
                above = down[half][tile + 1] if tile < tiles - 1 else last[half]
                axial = jnp.where(bottom, below, up[half][tile]) + jnp.where(top, above, down[half][tile])
                value = here[half][tile]
                inner = jnp.where(low, pltpu.roll(value, 1, 1), 0.0)
                outer = jnp.where(high, pltpu.roll(value, 127, 1), 0.0)
                sums[half].append((axial + inner) + outer)
        return sums

    def apply(scr, s, kind):
        near = beside(scr, s)
        for half in range(2):
            for tile in range(tiles):
                here = get(scr, s, half, tile)
                beyond = get(scr, s - 1, half, tile) + get(scr, s + 1, half, tile)
                diag = diag_scr[kind, s + 2, half, tile * 8 : tile * 8 + 8, :]
                yield half, tile, here, diag * here - (beyond + near[half][tile])

    def keep_diag(s, half, rows, sig):
        for i, mass in enumerate((mass_scale[0], mass_scale[3])):
            diag_scr[i, s + 2, half, rows, :] = 6.0 + mass * sig

    every, upper, lower = slice(0, NODES), slice(0, 24), slice(24, NODES)
    for half in range(2):
        for s in range(4):
            keep_diag(s, half, every, sig_ref[:, s * SLICE + half * 128 : s * SLICE + half * 128 + 128])
        for behind, first in ((True, -2), (False, 4)):
            for s in range(2):
                at = s * SLICE + half * 128
                sig = halo(behind, (slice(ROW, ROW + 24), slice(at, at + 128)))
                keep_diag(first + s, half, upper, sig)
                at = 2 * SLICE + half * 128
                sig = halo(behind, (slice(ROW + 8 * s, ROW + 8 * s + 8), slice(at, at + 128)))
                keep_diag(first + s, half, lower, sig)

    def channel_step(channel, _):
        scalar = channel == 3
        vector_numbers = chebyshev_numbers(mass_scale[0])
        scalar_numbers = chebyshev_numbers(mass_scale[3])
        _, one, two = [
            jnp.where(scalar, b, a).astype(F32) for a, b in zip(vector_numbers, scalar_numbers)
        ]
        invert = jnp.where(scalar, 1.0 / scalar_numbers[0], 1.0 / vector_numbers[0]).astype(F32)
        kind = jnp.where(scalar, 1, 0)
        base = channel * NODES

        def rows(tile):
            return pl.ds(pl.multiple_of(base + tile * 8, 8), 8)

        def source(s, half, tile):
            behind, beyond = s < 0, s < 0 or s > 3
            if beyond:
                s = s + 3 if behind else s - 4
            index = (rows(tile), slice(s * SLICE + half * 128, s * SLICE + half * 128 + 128))
            return halo(behind, index) if beyond else own_ref[index]

        for s in range(-3, 7):
            for half in range(2):
                for tile in range(tiles):
                    put(d_scr, s, half, tile, source(s, half, tile) * invert)
        for s in range(-2, 6):
            for half, tile, here, applied in apply(d_scr, s, kind):
                rest = source(s, half, tile) - applied
                put(y_scr, s, half, tile, here + (one * here + two * rest))
        for s in range(-1, 5):
            for half, tile, here, applied in apply(y_scr, s, kind):
                rest = source(s, half, tile) - applied
                put(p_scr, s, half, tile, rest * invert)
                if 0 <= s < 4:
                    keep_scr[s, half, tile * 8 : tile * 8 + 8, :] = rest
        for s in range(4):
            for half, tile, here, applied in apply(p_scr, s, kind):
                rest = keep_scr[s, half, tile * 8 : tile * 8 + 8, :] - applied
                at = s * SLICE + half * 128
                value = (get(y_scr, s, half, tile) + here) + (one * here + two * rest)
                sol_scr[rows(tile), at : at + 128] = value
        return 0

    lax.fori_loop(0, 4, channel_step, 0)
    for group in range(BLOCKS // 128):
        part = slice(group * 128, (group + 1) * 128)
        row_scr[part, :] = sol_scr[:, part].T
    to_scalar.wait()
    for slot in range(SLOTS):
        back_ref[slot : slot + 1, :] = row_scr[pl.ds(place_scr[slot // 128, slot % 128], 1), :]


def sweeps(own, far, near, sig, labels):
    vmem = pl.BlockSpec(memory_space=pltpu.VMEM)
    field = pltpu.VMEM((10, 2, NODES, 128), F32)
    return pl.pallas_call(
        sweeps_kernel,
        out_shape=jax.ShapeDtypeStruct((SLOTS, ROW), F32),
        in_specs=[vmem] * 5,
        out_specs=vmem,
        scratch_shapes=[
            pltpu.VMEM((2, 8, 2, NODES, 128), F32),
            field,
            field,
            field,
            pltpu.VMEM((4, 2, NODES, 128), F32),
            pltpu.VMEM((ROW, BLOCKS), F32),
            pltpu.VMEM((BLOCKS, ROW), F32),
            pltpu.SMEM((SLOTS // 128, 128), I32),
            pltpu.SemaphoreType.DMA,
        ],
        compiler_params=pltpu.CompilerParams(vmem_limit_bytes=VMEM_LIMIT),
        name="sweeps",
    )(own, far, near, sig, labels)


def lift_kernel(got_ref, slot_ref, res_ref, tan_ref, jac_ref, ends_ref, out_hbm, row_scr, y_scr, out_ref, out_sem):
    def take(group, step):
        for inner in range(16):
            block = group * 128 + step * 16 + inner
            row_scr[block : block + 1, :] = got_ref[pl.ds(slot_ref[0, block], 1), :]

    def turn(group):
        y_scr[group] = row_scr[group * 128 : (group + 1) * 128, :].T

    groups = BLOCKS // 128
    for step in range(8):
        take(0, step)
    turn(0)
    for group in range(groups):
        lanes = slice(group * 128, (group + 1) * 128)

        def pick(channel, low, quarter):
            parts = [
                jnp.take_along_axis(y_scr[group, channel * NODES + 8 * k : channel * NODES + 8 * k + 8, :], low, axis=0)
                for k in range(4)
            ]
            return jnp.where(
                quarter < 2,
                jnp.where(quarter == 0, parts[0], parts[1]),
                jnp.where(quarter == 2, parts[2], parts[3]),
            )

        for step in range(EDGES // 8):
            if group + 1 < groups:
                take(group + 1, step)
            edges = slice(step * 8, (step + 1) * 8)
            tail = ends_ref[0, edges, lanes]
            head = ends_ref[1, edges, lanes]
            tail_at = (tail & 7, tail >> 3)
            head_at = (head & 7, head >> 3)
            total = pick(3, *head_at) - pick(3, *tail_at)
            for channel in range(3):
                pair = pick(channel, *head_at) + pick(channel, *tail_at)
                total = total + 0.5 * tan_ref[channel, edges, lanes] * pair
            out_ref[edges, lanes] = jac_ref[edges, lanes] * res_ref[edges, lanes] + total
        if group + 1 < groups:
            turn(group + 1)
        pltpu.make_async_copy(out_ref.at[:, lanes], out_hbm.at[:, lanes], out_sem.at[group]).start()
    for group in range(groups):
        lanes = slice(group * 128, (group + 1) * 128)
        pltpu.make_async_copy(out_ref.at[:, lanes], out_hbm.at[:, lanes], out_sem.at[group]).wait()


def lift(got, slots, residual, tangent, jacobi, ends):
    vmem = pl.BlockSpec(memory_space=pltpu.VMEM)
    return pl.pallas_call(
        lift_kernel,
        out_shape=jax.ShapeDtypeStruct((EDGES, BLOCKS), F32),
        in_specs=[vmem, pl.BlockSpec(memory_space=pltpu.SMEM), vmem, vmem, vmem, vmem],
        out_specs=pl.BlockSpec(memory_space=pltpu.HBM),
        scratch_shapes=[
            pltpu.VMEM((BLOCKS, ROW), F32),
            pltpu.VMEM((BLOCKS // 128, ROW, 128), F32),
            pltpu.VMEM((EDGES, BLOCKS), F32),
            pltpu.SemaphoreType.DMA((BLOCKS // 128,)),
        ],
        compiler_params=pltpu.CompilerParams(vmem_limit_bytes=VMEM_LIMIT),
        name="lift",
    )(got, slots, residual, tangent, jacobi, ends)


def exchange(rows):
    parts = rows.reshape(DEVICES, CAP, ROW)
    return lax.all_to_all(parts, RING, split_axis=0, concat_axis=0, tiled=True).reshape(SLOTS, ROW)


def per_device(residual, tangent, jacobi, ends, target, node_block, sigma):
    slabs = range(DEVICES)
    between = [(place(s), place((s + 1 if s % 2 else s - 1) % DEVICES)) for s in slabs]
    within = [(place(s), place(s ^ 1)) for s in slabs]
    sig_own = lax.ppermute(sigma, RING, [(s, place(s)) for s in slabs])
    send, slots = edge_terms(
        residual, tangent, ends, target.reshape(1, BLOCKS), node_block.reshape(1, BLOCKS)
    )
    got = exchange(send)
    own, far, near, labels, sig = block_sums(got, sig_own)
    far = lax.ppermute(far, RING, between)
    near = lax.ppermute(near, RING, within)
    back = sweeps(own, far, near, sig, labels)
    mine = exchange(back)
    return lift(mine, slots, residual, tangent, jacobi, ends)


def solution(mesh):
    in_specs = (
        P(None, RING),
        P(None, None, RING),
        P(None, RING),
        P(None, None, RING),
        P(RING, None),
        P(RING),
        P(RING, None, None),
    )
    return jax.shard_map(
        per_device, mesh=mesh, in_specs=in_specs, out_specs=P(None, RING), check_vma=False
    )
```

```python
import jax
import jax.numpy as jnp
from jax import lax
from jax.experimental import pallas as pl
from jax.experimental.pallas import tpu as pltpu
from jax.sharding import PartitionSpec as P

F32 = jnp.float32
BF16 = jnp.bfloat16
I32 = jnp.int32

EDGES = 64
NODES = 32
ROW = 4 * NODES
BLOCKS = 1024
CAP = 16
DEVICES = 128
SLOTS = DEVICES * CAP
SLICE = 256
HALO = 3 * SLICE
LABEL = 3 * NODES
RING = ("edge", "node")
VMEM_LIMIT = 24 * 1024 * 1024
FIRST_LIMIT = 60 * 1024 * 1024
MESSAGE = ROW + 16
TILES = NODES // 8

mass_scale = (1.0, 1.0, 1.0, 0.5)


def chebyshev_numbers(scale):
    upper = 12.0 + 8.0 * scale
    lower = upper / 8.0
    centre = (upper + lower) / 2.0
    radius = (upper - lower) / 2.0
    ratio = centre / radius
    first = 1.0 / ratio
    second = 1.0 / (2.0 * ratio - first)
    return (centre, second * first, 2.0 * second / radius)


def place(slab):
    return slab ^ (24 * ((slab >> 5) & 1)) ^ (6 * ((slab >> 3) & 1))


def odd_slab():
    return lax.axis_index("node") & 1


def split(value):
    high = value.astype(BF16)
    return high, (value - high.astype(F32)).astype(BF16)


def one_hot(mask):
    return jnp.where(mask, 1.0, 0.0).astype(BF16)


def iota(shape, dim):
    return lax.broadcasted_iota(I32, shape, dim)


def dot(left, right, dims):
    return lax.dot_general(left, right, (dims, ((), ())), preferred_element_type=F32)


def terms_kernel(
    target_hbm, block_hbm, res_hbm, tan_hbm, ends_hbm, send_hbm, slot_hbm,
    target_scr, block_scr, res_scr, tan_scr, ends_scr, term_scr, acc_scr, row_scr, send_scr, slot_ref, label_scr, place_scr,
    place_sem, list_sem, in_sem, out_sem,
):
    groups = BLOCKS // 128

    chunks = ((0, 128), (128, 128), (256, BLOCKS - 256))

    def fetch(chunk):
        lanes = pl.ds(*chunks[chunk])
        return [
            pltpu.make_async_copy(hbm.at[..., lanes], scr.at[..., lanes], in_sem.at[i, chunk])
            for i, (hbm, scr) in enumerate(((ends_hbm, ends_scr), (res_hbm, res_scr), (tan_hbm, tan_scr)))
        ]

    lists = [
        pltpu.make_async_copy(target_hbm, target_scr, list_sem.at[0]),
        pltpu.make_async_copy(block_hbm, block_scr, list_sem.at[1]),
    ]
    fetched = [fetch(chunk) for chunk in range(3)]
    for copy in fetched[0] + lists + fetched[1] + fetched[2]:
        copy.start()
    send_scr[...] = jnp.zeros((SLOTS, ROW), F32)
    node = iota((NODES, 128), 0)

    def turn(group):
        lanes = pl.ds(pl.multiple_of(group * 128, 128), 128)
        acc_scr[group, LABEL : LABEL + 1, :] = label_scr[:, lanes]
        row_scr[lanes, :] = acc_scr[group].T

    def post(group, step):
        for inner in range(16):
            block = group * 128 + step * 16 + inner
            send_scr[pl.ds(place_scr[0, block], 1), :] = row_scr[pl.ds(block, 1), :]

    def edge_step(step, lanes, sums):
        sums = list(sums)
        for inner in range(8):
            row = slice(inner, inner + 1)
            head = ends_scr[1, step, row, lanes] == node
            tail = ends_scr[0, step, row, lanes] == node
            either = head | tail
            value = res_scr[step, row, lanes]
            for channel in range(3):
                term = term_scr[channel, step, row, :]
                sums[channel] = sums[channel] + jnp.where(either, term, 0.0)
            sums[3] = sums[3] + jnp.where(head, value, jnp.where(tail, -value, 0.0))
        return tuple(sums)

    def lanes_step(group, turned, posted):
        lanes = pl.ds(pl.multiple_of(group * 128, 128), 128)
        term_scr[...] = 0.5 * tan_scr[:, :, :, lanes] * res_scr[:, :, lanes][None]
        if turned:
            turn(group - 1)
        if posted:
            post(group - 2, 0)
        sums = edge_step(0, lanes, (jnp.zeros((NODES, 128), F32),) * 4)

        def tile_step(step, sums):
            if posted:
                post(group - 2, step)
            return edge_step(step, lanes, sums)

        sums = lax.fori_loop(1, EDGES // 8, tile_step, sums)
        for channel in range(3):
            acc_scr[group, channel * NODES : (channel + 1) * NODES, :] = sums[channel]
        acc_scr[group, LABEL:, :] = sums[3]

    for copy in fetched[0]:
        copy.wait()
    lanes_step(0, False, False)
    for copy in lists:
        copy.wait()

    holder = place(target_scr[...])
    device = iota((DEVICES, 128), 0)
    before = one_hot(iota((128, 128), 0) < iota((128, 128), 1))
    seen = jnp.zeros((DEVICES, 1), F32)
    for group in range(groups):
        lanes = slice(group * 128, (group + 1) * 128)
        same = holder[:, lanes] == device
        hot = jnp.where(same, 1.0, 0.0)
        count = dot(hot.astype(BF16), before, ((1,), (0,))) + seen
        rank = jnp.sum(jnp.where(same, count, 0.0), axis=0, keepdims=True)
        slot_ref[:, lanes] = holder[:, lanes] * CAP + rank.astype(I32)
        seen = seen + jnp.sum(hot, axis=1, keepdims=True)
    to_scalar = pltpu.make_async_copy(slot_ref, place_scr, place_sem.at[0])
    to_scalar.start()
    to_lift = pltpu.make_async_copy(slot_ref, slot_hbm, place_sem.at[1])
    to_lift.start()

    number = block_scr[...]
    label = (number & ~255) + (number & 7) * 32 + ((number >> 3) & 31)
    label = (label + 1).astype(F32)
    label_scr[...] = label

    for copy in fetched[1]:
        copy.wait()
    lanes_step(1, True, False)
    for copy in fetched[2]:
        copy.wait()
    to_scalar.wait()

    def group_step(group, _):
        lanes_step(group, True, True)
        return 0

    lax.fori_loop(2, groups, group_step, 0)
    turn(groups - 1)
    for group in (groups - 2, groups - 1):
        for step in range(8):
            post(group, step)
    parts = 8
    out = []
    for part in range(parts):
        rows = pl.ds(part * (SLOTS // parts), SLOTS // parts)
        out.append(pltpu.make_async_copy(send_scr.at[rows, :], send_hbm.at[rows, :], out_sem.at[part]))
    for copy in out:
        copy.start()
    for copy in out:
        copy.wait()
    to_lift.wait()


def edge_terms(residual, tangent, ends, target, node_block):
    tiles = EDGES // 8
    hbm = pl.BlockSpec(memory_space=pltpu.HBM)
    return pl.pallas_call(
        terms_kernel,
        out_shape=(
            jax.ShapeDtypeStruct((SLOTS, ROW), F32),
            jax.ShapeDtypeStruct((1, BLOCKS), I32),
        ),
        in_specs=[hbm] * 5,
        out_specs=[hbm, hbm],
        scratch_shapes=[
            pltpu.VMEM((1, BLOCKS), I32),
            pltpu.VMEM((1, BLOCKS), I32),
            pltpu.VMEM((tiles, 8, BLOCKS), F32),
            pltpu.VMEM((3, tiles, 8, BLOCKS), F32),
            pltpu.VMEM((2, tiles, 8, BLOCKS), I32),
            pltpu.VMEM((3, tiles, 8, 128), F32),
            pltpu.VMEM((BLOCKS // 128, ROW, 128), F32),
            pltpu.VMEM((BLOCKS, ROW), F32),
            pltpu.VMEM((SLOTS, ROW), F32),
            pltpu.VMEM((1, BLOCKS), I32),
            pltpu.VMEM((1, BLOCKS), F32),
            pltpu.SMEM((1, BLOCKS), I32),
            pltpu.SemaphoreType.DMA((2,)),
            pltpu.SemaphoreType.DMA((2,)),
            pltpu.SemaphoreType.DMA((3, 3)),
            pltpu.SemaphoreType.DMA((8,)),
        ],
        compiler_params=pltpu.CompilerParams(vmem_limit_bytes=FIRST_LIMIT),
        cost_estimate=pl.CostEstimate(flops=50_000_000, bytes_accessed=20_000_000, transcendentals=0),
        name="edge_terms",
    )(
        target,
        node_block,
        residual.reshape(tiles, 8, BLOCKS),
        tangent.reshape(3, tiles, 8, BLOCKS),
        ends.reshape(2, tiles, 8, BLOCKS),
    )


def numbers(scalar):
    centre, one, two = chebyshev_numbers(mass_scale[3 if scalar else 0])
    return 1.0 / centre, one, two, mass_scale[3 if scalar else 0]


def beside(here):
    lane = iota((8, 128), 1)
    row = iota((8, 128), 0)
    low, high = (lane & 31) > 0, (lane & 31) < 31
    bottom, top = row == 0, row == 7
    up = [[pltpu.roll(value, 1, 0) for value in part] for part in here]
    down = [[pltpu.roll(value, 7, 0) for value in part] for part in here]
    first = [pltpu.roll(part[-1], 32, 1) for part in up]
    last = [pltpu.roll(part[0], 96, 1) for part in down]
    first = [jnp.where(lane < 32, 0.0, first[0]), jnp.where(lane < 32, first[0], first[1])]
    last = [jnp.where(lane < 96, last[0], last[1]), jnp.where(lane < 96, last[1], 0.0)]
    sums = []
    for half in range(2):
        sums.append([])
        for tile in range(TILES):
            below = up[half][tile - 1] if tile else first[half]
            above = down[half][tile + 1] if tile < TILES - 1 else last[half]
            axial = jnp.where(bottom, below, up[half][tile]) + jnp.where(top, above, down[half][tile])
            value = here[half][tile]
            inner = jnp.where(low, pltpu.roll(value, 1, 1), 0.0)
            outer = jnp.where(high, pltpu.roll(value, 127, 1), 0.0)
            sums[half].append((axial + inner) + outer)
    return sums


def spot(s, half):
    return slice(s * SLICE + half * 128, s * SLICE + half * 128 + 128)


def summed(rows_scr, hot):
    both = dot(rows_scr[...], hot, ((1,), (0,)))
    sums = both[:ROW] + both[ROW:]
    first = iota((NODES, SLICE), 0) == 0
    scalar = sums[LABEL:]
    rest = -jnp.sum(jnp.where(first, 0.0, scalar), axis=0, keepdims=True)
    return jnp.concatenate([sums[:LABEL], jnp.where(first, rest, scalar)], axis=0)


def turned_label(label):
    return (label.astype(I32) - 1) ^ (odd_slab() * 768)


def first_sweep(source, sigma, store, s, inside):
    for channel in range(4):
        invert, one, two, mass = numbers(channel == 3)
        here = [
            [source(channel, s, half, tile) * invert for tile in range(TILES)] for half in range(2)
        ]
        near = beside(here)
        for half in range(2):
            for tile in range(TILES):
                around = near[half][tile]
                for other in inside:
                    around = around + source(channel, other, half, tile) * invert
                value = here[half][tile]
                rest = source(channel, s, half, tile) - (
                    (6.0 + mass * sigma(s, half, tile)) * value - around
                )
                store(channel, half, tile, value + (one * value + two * rest))


def put_sigma(message_ref, sig_ref, s):
    for tile in range(TILES):
        at, lanes = ROW + tile // 3 * 8, slice(tile % 3 * SLICE, (tile % 3 + 1) * SLICE)
        message_ref[at : at + 8, lanes] = sig_ref[tile * 8 : tile * 8 + 8, s * SLICE : (s + 1) * SLICE]
    message_ref[ROW + 8 :, SLICE:] = jnp.zeros((8, 2 * SLICE), F32)


def channel_rows(channel, tile):
    at = channel * NODES + tile * 8
    return slice(at, at + 8)


def far_kernel(got_ref, sigma_ref, far_ref, mid_ref, from_ref, sig_ref, rows_scr, hot_scr):
    for s in range(4):
        turned = sigma_ref[s ^ (odd_slab() * 3)].T
        for block in range(8):
            at = s * SLICE + block * 32
            sig_ref[:, at : at + 32] = turned[block * 32 : (block + 1) * 32, :]
    for step in range(SLOTS // 128):
        part = slice(step * 128, (step + 1) * 128)
        turned = got_ref[part, :].T
        high, low = split(turned)
        rows_scr[0:ROW, part] = high
        rows_scr[ROW:, part] = low
        from_ref[step : step + 1, :] = jnp.maximum(turned_label(turned[LABEL : LABEL + 1, :]), 0)
        column = turned_label(got_ref[part, LABEL : LABEL + 1])
        hot_scr[part, :] = one_hot(column == iota((128, HALO), 1))

    def source(channel, s, half, tile):
        if s == 0:
            return far_ref[channel_rows(channel, tile), spot(0, half)]
        return mid_ref[channel_rows(channel, tile), spot(s - 1, half)]

    def sigma(s, half, tile):
        return sig_ref[tile * 8 : tile * 8 + 8, spot(s, half)]

    def store(s):
        def one(channel, half, tile, value):
            far_ref[channel_rows(channel, tile), spot(1 + s, half)] = value

        return one

    for s in range(3):
        sums = summed(rows_scr, hot_scr[:, s * SLICE : (s + 1) * SLICE])
        if s == 0:
            far_ref[0:ROW, 0:SLICE] = sums
        else:
            mid_ref[:, (s - 1) * SLICE : s * SLICE] = sums
    first_sweep(source, sigma, store(0), 0, (1,))
    first_sweep(source, sigma, store(1), 1, (0, 2))
    put_sigma(far_ref, sig_ref, 0)


def far_sums(got, sigma):
    vmem = pl.BlockSpec(memory_space=pltpu.VMEM)
    return pl.pallas_call(
        far_kernel,
        out_shape=(
            jax.ShapeDtypeStruct((MESSAGE, HALO), F32),
            jax.ShapeDtypeStruct((ROW, 2 * SLICE), F32),
            jax.ShapeDtypeStruct((SLOTS // 128, 128), I32),
            jax.ShapeDtypeStruct((NODES, BLOCKS), F32),
        ),
        in_specs=[vmem] * 2,
        out_specs=[vmem] * 4,
        scratch_shapes=[
            pltpu.VMEM((2 * ROW, SLOTS), BF16),
            pltpu.VMEM((SLOTS, HALO), BF16),
        ],
        compiler_params=pltpu.CompilerParams(vmem_limit_bytes=VMEM_LIMIT),
        cost_estimate=pl.CostEstimate(flops=800_000_000, bytes_accessed=5_000_000, transcendentals=0),
        name="far_sums",
    )(got, sigma)


def near_kernel(got_ref, mid_ref, sig_ref, near_ref, rows_scr, hot_scr):
    for step in range(SLOTS // 128):
        part = slice(step * 128, (step + 1) * 128)
        high, low = split(got_ref[part, :].T)
        rows_scr[0:ROW, part] = high
        rows_scr[ROW:, part] = low
        column = turned_label(got_ref[part, LABEL : LABEL + 1])
        hot_scr[part, :] = one_hot(column == iota((128, SLICE), 1) + HALO)

    def source(channel, s, half, tile):
        if s == 3:
            return near_ref[channel_rows(channel, tile), spot(0, half)]
        return mid_ref[channel_rows(channel, tile), spot(s - 1, half)]

    def sigma(s, half, tile):
        return sig_ref[tile * 8 : tile * 8 + 8, spot(s, half)]

    def store(s):
        def one(channel, half, tile, value):
            near_ref[channel_rows(channel, tile), spot(4 - s, half)] = value

        return one

    near_ref[0:ROW, 0:SLICE] = summed(rows_scr, hot_scr[...])
    first_sweep(source, sigma, store(3), 3, (2,))
    first_sweep(source, sigma, store(2), 2, (1, 3))
    put_sigma(near_ref, sig_ref, 3)


def near_sums(got, mid, sig):
    vmem = pl.BlockSpec(memory_space=pltpu.VMEM)
    return pl.pallas_call(
        near_kernel,
        out_shape=jax.ShapeDtypeStruct((MESSAGE, HALO), F32),
        in_specs=[vmem] * 3,
        out_specs=vmem,
        scratch_shapes=[
            pltpu.VMEM((2 * ROW, SLOTS), BF16),
            pltpu.VMEM((SLOTS, SLICE), BF16),
        ],
        compiler_params=pltpu.CompilerParams(vmem_limit_bytes=VMEM_LIMIT),
        cost_estimate=pl.CostEstimate(flops=300_000_000, bytes_accessed=4_000_000, transcendentals=0),
        name="near_sums",
    )(got, mid, sig)


def sweeps_kernel(
    far_ref, near_ref, mid_ref, before_ref, after_ref, sig_ref, from_ref, back_ref,
    diag_scr, y_scr, p_scr, keep_scr, sol_scr, row_scr, place_scr, place_sem,
):
    to_scalar = pltpu.make_async_copy(from_ref, place_scr, place_sem)
    to_scalar.start()

    def put(scr, s, half, tile, value):
        scr[s + 2, half, tile * 8 : tile * 8 + 8, :] = value

    def get(scr, s, half, tile):
        return scr[s + 2, half, tile * 8 : tile * 8 + 8, :]

    def apply(scr, s, kind):
        near = beside([[get(scr, s, half, tile) for tile in range(TILES)] for half in range(2)])
        for half in range(2):
            for tile in range(TILES):
                here = get(scr, s, half, tile)
                beyond = get(scr, s - 1, half, tile) + get(scr, s + 1, half, tile)
                diag = diag_scr[kind, s + 1, half, tile * 8 : tile * 8 + 8, :]
                yield half, tile, here, diag * here - (beyond + near[half][tile])

    for half in range(2):
        for tile in range(TILES):
            nodes = slice(tile * 8, tile * 8 + 8)
            at = ROW + tile // 3 * 8
            for s in range(-1, 5):
                if 0 <= s < 4:
                    sigma = sig_ref[nodes, spot(s, half)]
                else:
                    sigma = (before_ref if s < 0 else after_ref)[at : at + 8, spot(tile % 3, half)]
                for i, mass in enumerate((mass_scale[0], mass_scale[3])):
                    diag_scr[i, s + 1, half, nodes, :] = 6.0 + mass * sigma

    def channel_step(channel, _):
        scalar = channel == 3
        invert, one, two, _ = [
            jnp.where(scalar, b, a).astype(F32) for a, b in zip(numbers(False), numbers(True))
        ]
        kind = jnp.where(scalar, 1, 0)
        base = channel * NODES
        across = two * invert

        def rows(tile):
            return pl.ds(pl.multiple_of(base + tile * 8, 8), 8)

        def source(s, half, tile):
            if s in (1, 2):
                return mid_ref[rows(tile), spot(s - 1, half)]
            ref = {-1: before_ref, 0: far_ref, 3: near_ref, 4: after_ref}[s]
            return ref[rows(tile), spot(0, half)]

        for half in range(2):
            for tile in range(TILES):
                for s, ref, beyond in ((0, far_ref, -1), (3, near_ref, 4), (-1, before_ref, 0), (4, after_ref, 3)):
                    part = ref[rows(tile), spot(1, half)]
                    put(y_scr, s, half, tile, part + across * source(beyond, half, tile))
                for s, ref in ((1, far_ref), (2, near_ref), (-2, before_ref), (5, after_ref)):
                    put(y_scr, s, half, tile, ref[rows(tile), spot(2, half)])
        for s in range(-1, 5):
            for half, tile, here, applied in apply(y_scr, s, kind):
                rest = source(s, half, tile) - applied
                put(p_scr, s, half, tile, rest * invert)
                if 0 <= s < 4:
                    keep_scr[s, half, tile * 8 : tile * 8 + 8, :] = rest
        for s in range(4):
            for half, tile, here, applied in apply(p_scr, s, kind):
                rest = keep_scr[s, half, tile * 8 : tile * 8 + 8, :] - applied
                value = (get(y_scr, s, half, tile) + here) + (one * here + two * rest)
                sol_scr[rows(tile), spot(s, half)] = value
        return 0

    lax.fori_loop(0, 4, channel_step, 0)
    for group in range(BLOCKS // 128):
        part = slice(group * 128, (group + 1) * 128)
        row_scr[part, :] = sol_scr[:, part].T
    to_scalar.wait()
    for slot in range(SLOTS):
        back_ref[slot : slot + 1, :] = row_scr[pl.ds(place_scr[slot // 128, slot % 128], 1), :]


def sweeps(far, near, mid, before, after, sig, labels):
    vmem = pl.BlockSpec(memory_space=pltpu.VMEM)
    field = pltpu.VMEM((8, 2, NODES, 128), F32)
    return pl.pallas_call(
        sweeps_kernel,
        out_shape=jax.ShapeDtypeStruct((SLOTS, ROW), F32),
        in_specs=[vmem] * 7,
        out_specs=vmem,
        scratch_shapes=[
            pltpu.VMEM((2, 6, 2, NODES, 128), F32),
            field,
            field,
            pltpu.VMEM((4, 2, NODES, 128), F32),
            pltpu.VMEM((ROW, BLOCKS), F32),
            pltpu.VMEM((BLOCKS, ROW), F32),
            pltpu.SMEM((SLOTS // 128, 128), I32),
            pltpu.SemaphoreType.DMA,
        ],
        compiler_params=pltpu.CompilerParams(vmem_limit_bytes=VMEM_LIMIT),
        name="sweeps",
    )(far, near, mid, before, after, sig, labels)


def lift_kernel(got_ref, slot_ref, res_ref, tan_ref, jac_ref, ends_ref, out_hbm, row_scr, y_scr, out_ref, out_sem):
    def take(group, step):
        for inner in range(16):
            block = group * 128 + step * 16 + inner
            row_scr[block : block + 1, :] = got_ref[pl.ds(slot_ref[0, block], 1), :]

    def turn(group):
        y_scr[group] = row_scr[group * 128 : (group + 1) * 128, :].T

    groups = BLOCKS // 128
    for step in range(8):
        take(0, step)
    turn(0)
    for group in range(groups):
        lanes = slice(group * 128, (group + 1) * 128)

        def pick(channel, low, quarter):
            parts = [
                jnp.take_along_axis(y_scr[group, channel * NODES + 8 * k : channel * NODES + 8 * k + 8, :], low, axis=0)
                for k in range(4)
            ]
            return jnp.where(
                quarter < 2,
                jnp.where(quarter == 0, parts[0], parts[1]),
                jnp.where(quarter == 2, parts[2], parts[3]),
            )

        for step in range(EDGES // 8):
            if group + 1 < groups:
                take(group + 1, step)
            edges = slice(step * 8, (step + 1) * 8)
            tail = ends_ref[0, edges, lanes]
            head = ends_ref[1, edges, lanes]
            tail_at = (tail & 7, tail >> 3)
            head_at = (head & 7, head >> 3)
            total = pick(3, *head_at) - pick(3, *tail_at)
            for channel in range(3):
                pair = pick(channel, *head_at) + pick(channel, *tail_at)
                total = total + 0.5 * tan_ref[channel, edges, lanes] * pair
            out_ref[edges, lanes] = jac_ref[edges, lanes] * res_ref[edges, lanes] + total
        if group + 1 < groups:
            turn(group + 1)
        pltpu.make_async_copy(out_ref.at[:, lanes], out_hbm.at[:, lanes], out_sem.at[group]).start()
    for group in range(groups):
        lanes = slice(group * 128, (group + 1) * 128)
        pltpu.make_async_copy(out_ref.at[:, lanes], out_hbm.at[:, lanes], out_sem.at[group]).wait()


def lift(got, slots, residual, tangent, jacobi, ends):
    vmem = pl.BlockSpec(memory_space=pltpu.VMEM)
    return pl.pallas_call(
        lift_kernel,
        out_shape=jax.ShapeDtypeStruct((EDGES, BLOCKS), F32),
        in_specs=[vmem, pl.BlockSpec(memory_space=pltpu.SMEM), vmem, vmem, vmem, vmem],
        out_specs=pl.BlockSpec(memory_space=pltpu.HBM),
        scratch_shapes=[
            pltpu.VMEM((BLOCKS, ROW), F32),
            pltpu.VMEM((BLOCKS // 128, ROW, 128), F32),
            pltpu.VMEM((EDGES, BLOCKS), F32),
            pltpu.SemaphoreType.DMA((BLOCKS // 128,)),
        ],
        compiler_params=pltpu.CompilerParams(vmem_limit_bytes=VMEM_LIMIT),
        name="lift",
    )(got, slots, residual, tangent, jacobi, ends)


def exchange(rows):
    parts = rows.reshape(DEVICES, CAP, ROW)
    return lax.all_to_all(parts, RING, split_axis=0, concat_axis=0, tiled=True).reshape(SLOTS, ROW)


def per_device(residual, tangent, jacobi, ends, target, node_block, sigma):
    slabs = range(DEVICES)
    between = [(place(s), place((s + 1 if s % 2 else s - 1) % DEVICES)) for s in slabs]
    within = [(place(s), place(s ^ 1)) for s in slabs]
    sig_own = lax.ppermute(sigma, RING, [(s, place(s)) for s in slabs])
    send, slots = edge_terms(
        residual, tangent, ends, target.reshape(1, BLOCKS), node_block.reshape(1, BLOCKS)
    )
    got = exchange(send)
    far, mid, labels, sig = far_sums(got, sig_own)
    before = lax.ppermute(far, RING, between)
    near = near_sums(got, mid, sig)
    after = lax.ppermute(near, RING, within)
    back = sweeps(far, near, mid, before, after, sig, labels)
    mine = exchange(back)
    return lift(mine, slots, residual, tangent, jacobi, ends)


def solution(mesh):
    in_specs = (
        P(None, RING),
        P(None, None, RING),
        P(None, RING),
        P(None, None, RING),
        P(RING, None),
        P(RING),
        P(RING, None, None),
    )
    return jax.shard_map(
        per_device, mesh=mesh, in_specs=in_specs, out_specs=P(None, RING), check_vma=False
    )
```

```python
import jax
import jax.numpy as jnp
from jax import lax
from jax.experimental import pallas as pl
from jax.experimental.pallas import tpu as pltpu
from jax.sharding import PartitionSpec as P

F32 = jnp.float32
BF16 = jnp.bfloat16
I32 = jnp.int32

EDGES = 64
NODES = 32
ROW = 4 * NODES
BLOCKS = 1024
CAP = 16
DEVICES = 128
SLOTS = DEVICES * CAP
SLICE = 256
HALO = 3 * SLICE
LABEL = 3 * NODES
RING = ("edge", "node")
VMEM_LIMIT = 24 * 1024 * 1024
FIRST_LIMIT = 60 * 1024 * 1024
MESSAGE = ROW + 16
TILES = NODES // 8

mass_scale = (1.0, 1.0, 1.0, 0.5)


def chebyshev_numbers(scale):
    upper = 12.0 + 8.0 * scale
    lower = upper / 8.0
    centre = (upper + lower) / 2.0
    radius = (upper - lower) / 2.0
    ratio = centre / radius
    first = 1.0 / ratio
    second = 1.0 / (2.0 * ratio - first)
    return (centre, second * first, 2.0 * second / radius)


def place(slab):
    return slab ^ (24 * ((slab >> 5) & 1)) ^ (6 * ((slab >> 3) & 1))


def odd_slab():
    return lax.axis_index("node") & 1


def split(value):
    high = value.astype(BF16)
    return high, (value - high.astype(F32)).astype(BF16)


def one_hot(mask):
    return jnp.where(mask, 1.0, 0.0).astype(BF16)


def iota(shape, dim):
    return lax.broadcasted_iota(I32, shape, dim)


def dot(left, right, dims):
    return lax.dot_general(left, right, (dims, ((), ())), preferred_element_type=F32)


def terms_kernel(
    target_hbm, block_hbm, res_hbm, tan_hbm, ends_hbm, send_hbm, slot_hbm,
    target_scr, block_scr, res_scr, tan_scr, ends_scr, term_scr, acc_scr, row_scr, send_scr, slot_ref, label_scr, place_scr,
    place_sem, list_sem, in_sem, out_sem,
):
    groups = BLOCKS // 128

    chunks = ((0, 128), (128, 128), (256, BLOCKS - 256))

    def fetch(chunk):
        lanes = pl.ds(*chunks[chunk])
        return [
            pltpu.make_async_copy(hbm.at[..., lanes], scr.at[..., lanes], in_sem.at[i, chunk])
            for i, (hbm, scr) in enumerate(((ends_hbm, ends_scr), (res_hbm, res_scr), (tan_hbm, tan_scr)))
        ]

    lists = [
        pltpu.make_async_copy(target_hbm, target_scr, list_sem.at[0]),
        pltpu.make_async_copy(block_hbm, block_scr, list_sem.at[1]),
    ]
    fetched = [fetch(chunk) for chunk in range(3)]
    for copy in fetched[0] + lists + fetched[1] + fetched[2]:
        copy.start()
    send_scr[...] = jnp.zeros((SLOTS, ROW), F32)
    node = iota((NODES, 128), 0)

    def turn(group):
        lanes = pl.ds(pl.multiple_of(group * 128, 128), 128)
        acc_scr[group, LABEL : LABEL + 1, :] = label_scr[:, lanes]
        row_scr[lanes, :] = acc_scr[group].T

    def post(group, step):
        for inner in range(16):
            block = group * 128 + step * 16 + inner
            send_scr[pl.ds(place_scr[0, block], 1), :] = row_scr[pl.ds(block, 1), :]

    def edge_step(step, lanes, sums):
        sums = list(sums)
        for inner in range(8):
            row = slice(inner, inner + 1)
            head = ends_scr[1, step, row, lanes] == node
            tail = ends_scr[0, step, row, lanes] == node
            either = head | tail
            value = res_scr[step, row, lanes]
            for channel in range(3):
                term = term_scr[channel, step, row, :]
                sums[channel] = sums[channel] + jnp.where(either, term, 0.0)
            sums[3] = sums[3] + jnp.where(head, value, jnp.where(tail, -value, 0.0))
        return tuple(sums)

    def lanes_step(group, turned, posted):
        lanes = pl.ds(pl.multiple_of(group * 128, 128), 128)
        term_scr[...] = 0.5 * tan_scr[:, :, :, lanes] * res_scr[:, :, lanes][None]
        if turned:
            turn(group - 1)
        sums = (jnp.zeros((NODES, 128), F32),) * 4
        for step in range(3):
            if posted:
                post(group - 2, step)
            sums = edge_step(step, lanes, sums)

        def tile_step(step, sums):
            if posted:
                post(group - 2, step)
            return edge_step(step, lanes, sums)

        sums = lax.fori_loop(3, EDGES // 8, tile_step, sums)
        for channel in range(3):
            acc_scr[group, channel * NODES : (channel + 1) * NODES, :] = sums[channel]
        acc_scr[group, LABEL:, :] = sums[3]

    for copy in fetched[0]:
        copy.wait()
    lanes_step(0, False, False)
    for copy in lists:
        copy.wait()

    holder = place(target_scr[...])
    device = iota((DEVICES, 128), 0)
    before = one_hot(iota((128, 128), 0) < iota((128, 128), 1))
    seen = jnp.zeros((DEVICES, 1), F32)
    for group in range(groups):
        lanes = slice(group * 128, (group + 1) * 128)
        same = holder[:, lanes] == device
        hot = jnp.where(same, 1.0, 0.0)
        count = dot(hot.astype(BF16), before, ((1,), (0,))) + seen
        rank = jnp.sum(jnp.where(same, count, 0.0), axis=0, keepdims=True)
        slot_ref[:, lanes] = holder[:, lanes] * CAP + rank.astype(I32)
        seen = seen + jnp.sum(hot, axis=1, keepdims=True)
    to_scalar = pltpu.make_async_copy(slot_ref, place_scr, place_sem.at[0])
    to_scalar.start()
    to_lift = pltpu.make_async_copy(slot_ref, slot_hbm, place_sem.at[1])
    to_lift.start()

    number = block_scr[...]
    label = (number & ~255) + (number & 7) * 32 + ((number >> 3) & 31)
    label = (label + 1).astype(F32)
    label_scr[...] = label

    for copy in fetched[1]:
        copy.wait()
    lanes_step(1, True, False)
    for copy in fetched[2]:
        copy.wait()
    to_scalar.wait()

    def group_step(group, _):
        lanes_step(group, True, True)
        return 0

    lax.fori_loop(2, groups, group_step, 0)
    turn(groups - 1)
    for group in (groups - 2, groups - 1):
        for step in range(8):
            post(group, step)
    parts = 8
    out = []
    for part in range(parts):
        rows = pl.ds(part * (SLOTS // parts), SLOTS // parts)
        out.append(pltpu.make_async_copy(send_scr.at[rows, :], send_hbm.at[rows, :], out_sem.at[part]))
    for copy in out:
        copy.start()
    for copy in out:
        copy.wait()
    to_lift.wait()


def edge_terms(residual, tangent, ends, target, node_block):
    tiles = EDGES // 8
    hbm = pl.BlockSpec(memory_space=pltpu.HBM)
    return pl.pallas_call(
        terms_kernel,
        out_shape=(
            jax.ShapeDtypeStruct((SLOTS, ROW), F32),
            jax.ShapeDtypeStruct((1, BLOCKS), I32),
        ),
        in_specs=[hbm] * 5,
        out_specs=[hbm, hbm],
        scratch_shapes=[
            pltpu.VMEM((1, BLOCKS), I32),
            pltpu.VMEM((1, BLOCKS), I32),
            pltpu.VMEM((tiles, 8, BLOCKS), F32),
            pltpu.VMEM((3, tiles, 8, BLOCKS), F32),
            pltpu.VMEM((2, tiles, 8, BLOCKS), I32),
            pltpu.VMEM((3, tiles, 8, 128), F32),
            pltpu.VMEM((BLOCKS // 128, ROW, 128), F32),
            pltpu.VMEM((BLOCKS, ROW), F32),
            pltpu.VMEM((SLOTS, ROW), F32),
            pltpu.VMEM((1, BLOCKS), I32),
            pltpu.VMEM((1, BLOCKS), F32),
            pltpu.SMEM((1, BLOCKS), I32),
            pltpu.SemaphoreType.DMA((2,)),
            pltpu.SemaphoreType.DMA((2,)),
            pltpu.SemaphoreType.DMA((3, 3)),
            pltpu.SemaphoreType.DMA((8,)),
        ],
        compiler_params=pltpu.CompilerParams(vmem_limit_bytes=FIRST_LIMIT),
        cost_estimate=pl.CostEstimate(flops=50_000_000, bytes_accessed=20_000_000, transcendentals=0),
        name="edge_terms",
    )(
        target,
        node_block,
        residual.reshape(tiles, 8, BLOCKS),
        tangent.reshape(3, tiles, 8, BLOCKS),
        ends.reshape(2, tiles, 8, BLOCKS),
    )


def numbers(scalar):
    centre, one, two = chebyshev_numbers(mass_scale[3 if scalar else 0])
    return 1.0 / centre, one, two, mass_scale[3 if scalar else 0]


def beside(here):
    lane = iota((8, 128), 1)
    row = iota((8, 128), 0)
    low, high = (lane & 31) > 0, (lane & 31) < 31
    bottom, top = row == 0, row == 7
    up = [[pltpu.roll(value, 1, 0) for value in part] for part in here]
    down = [[pltpu.roll(value, 7, 0) for value in part] for part in here]
    first = [pltpu.roll(part[-1], 32, 1) for part in up]
    last = [pltpu.roll(part[0], 96, 1) for part in down]
    first = [jnp.where(lane < 32, 0.0, first[0]), jnp.where(lane < 32, first[0], first[1])]
    last = [jnp.where(lane < 96, last[0], last[1]), jnp.where(lane < 96, last[1], 0.0)]
    sums = []
    for half in range(2):
        sums.append([])
        for tile in range(TILES):
            below = up[half][tile - 1] if tile else first[half]
            above = down[half][tile + 1] if tile < TILES - 1 else last[half]
            axial = jnp.where(bottom, below, up[half][tile]) + jnp.where(top, above, down[half][tile])
            value = here[half][tile]
            inner = jnp.where(low, pltpu.roll(value, 1, 1), 0.0)
            outer = jnp.where(high, pltpu.roll(value, 127, 1), 0.0)
            sums[half].append((axial + inner) + outer)
    return sums


def spot(s, half):
    return slice(s * SLICE + half * 128, s * SLICE + half * 128 + 128)


def summed(rows_scr, hot):
    both = dot(rows_scr[...], hot, ((1,), (0,)))
    sums = both[:ROW] + both[ROW:]
    first = iota((NODES, SLICE), 0) == 0
    scalar = sums[LABEL:]
    rest = -jnp.sum(jnp.where(first, 0.0, scalar), axis=0, keepdims=True)
    return jnp.concatenate([sums[:LABEL], jnp.where(first, rest, scalar)], axis=0)


def turned_label(label):
    return (label.astype(I32) - 1) ^ (odd_slab() * 768)


def first_sweep(source, sigma, store, s, inside):
    for channel in range(4):
        invert, one, two, mass = numbers(channel == 3)
        here = [
            [source(channel, s, half, tile) * invert for tile in range(TILES)] for half in range(2)
        ]
        near = beside(here)
        for half in range(2):
            for tile in range(TILES):
                around = near[half][tile]
                for other in inside:
                    around = around + source(channel, other, half, tile) * invert
                value = here[half][tile]
                rest = source(channel, s, half, tile) - (
                    (6.0 + mass * sigma(s, half, tile)) * value - around
                )
                store(channel, half, tile, value + (one * value + two * rest))


def put_sigma(message_ref, sig_ref, s):
    for tile in range(TILES):
        at, lanes = ROW + tile // 3 * 8, slice(tile % 3 * SLICE, (tile % 3 + 1) * SLICE)
        message_ref[at : at + 8, lanes] = sig_ref[tile * 8 : tile * 8 + 8, s * SLICE : (s + 1) * SLICE]
    message_ref[ROW + 8 :, SLICE:] = jnp.zeros((8, 2 * SLICE), F32)


def channel_rows(channel, tile):
    at = channel * NODES + tile * 8
    return slice(at, at + 8)


def far_kernel(got_ref, sigma_ref, far_ref, mid_ref, from_ref, sig_ref, rows_scr, hot_scr):
    for s in range(4):
        turned = sigma_ref[s ^ (odd_slab() * 3)].T
        for block in range(8):
            at = s * SLICE + block * 32
            sig_ref[:, at : at + 32] = turned[block * 32 : (block + 1) * 32, :]
    for step in range(SLOTS // 128):
        part = slice(step * 128, (step + 1) * 128)
        turned = got_ref[part, :].T
        high, low = split(turned)
        rows_scr[0:ROW, part] = high
        rows_scr[ROW:, part] = low
        from_ref[step : step + 1, :] = jnp.maximum(turned_label(turned[LABEL : LABEL + 1, :]), 0)
        column = turned_label(got_ref[part, LABEL : LABEL + 1])
        hot_scr[part, :] = one_hot(column == iota((128, HALO), 1))

    def source(channel, s, half, tile):
        if s == 0:
            return far_ref[channel_rows(channel, tile), spot(0, half)]
        return mid_ref[channel_rows(channel, tile), spot(s - 1, half)]

    def sigma(s, half, tile):
        return sig_ref[tile * 8 : tile * 8 + 8, spot(s, half)]

    def store(s):
        def one(channel, half, tile, value):
            far_ref[channel_rows(channel, tile), spot(1 + s, half)] = value

        return one

    for s in range(3):
        sums = summed(rows_scr, hot_scr[:, s * SLICE : (s + 1) * SLICE])
        if s == 0:
            far_ref[0:ROW, 0:SLICE] = sums
        else:
            mid_ref[:, (s - 1) * SLICE : s * SLICE] = sums
    first_sweep(source, sigma, store(0), 0, (1,))
    first_sweep(source, sigma, store(1), 1, (0, 2))
    put_sigma(far_ref, sig_ref, 0)


def far_sums(got, sigma):
    vmem = pl.BlockSpec(memory_space=pltpu.VMEM)
    return pl.pallas_call(
        far_kernel,
        out_shape=(
            jax.ShapeDtypeStruct((MESSAGE, HALO), F32),
            jax.ShapeDtypeStruct((ROW, 2 * SLICE), F32),
            jax.ShapeDtypeStruct((SLOTS // 128, 128), I32),
            jax.ShapeDtypeStruct((NODES, BLOCKS), F32),
        ),
        in_specs=[vmem] * 2,
        out_specs=[vmem] * 4,
        scratch_shapes=[
            pltpu.VMEM((2 * ROW, SLOTS), BF16),
            pltpu.VMEM((SLOTS, HALO), BF16),
        ],
        compiler_params=pltpu.CompilerParams(vmem_limit_bytes=VMEM_LIMIT),
        cost_estimate=pl.CostEstimate(flops=800_000_000, bytes_accessed=5_000_000, transcendentals=0),
        name="far_sums",
    )(got, sigma)


def near_kernel(got_ref, mid_ref, sig_ref, near_ref, rows_scr, hot_scr):
    for step in range(SLOTS // 128):
        part = slice(step * 128, (step + 1) * 128)
        high, low = split(got_ref[part, :].T)
        rows_scr[0:ROW, part] = high
        rows_scr[ROW:, part] = low
        column = turned_label(got_ref[part, LABEL : LABEL + 1])
        hot_scr[part, :] = one_hot(column == iota((128, SLICE), 1) + HALO)

    def source(channel, s, half, tile):
        if s == 3:
            return near_ref[channel_rows(channel, tile), spot(0, half)]
        return mid_ref[channel_rows(channel, tile), spot(s - 1, half)]

    def sigma(s, half, tile):
        return sig_ref[tile * 8 : tile * 8 + 8, spot(s, half)]

    def store(s):
        def one(channel, half, tile, value):
            near_ref[channel_rows(channel, tile), spot(4 - s, half)] = value

        return one

    near_ref[0:ROW, 0:SLICE] = summed(rows_scr, hot_scr[...])
    first_sweep(source, sigma, store(3), 3, (2,))
    first_sweep(source, sigma, store(2), 2, (1, 3))
    put_sigma(near_ref, sig_ref, 3)


def near_sums(got, mid, sig):
    vmem = pl.BlockSpec(memory_space=pltpu.VMEM)
    return pl.pallas_call(
        near_kernel,
        out_shape=jax.ShapeDtypeStruct((MESSAGE, HALO), F32),
        in_specs=[vmem] * 3,
        out_specs=vmem,
        scratch_shapes=[
            pltpu.VMEM((2 * ROW, SLOTS), BF16),
            pltpu.VMEM((SLOTS, SLICE), BF16),
        ],
        compiler_params=pltpu.CompilerParams(vmem_limit_bytes=VMEM_LIMIT),
        cost_estimate=pl.CostEstimate(flops=300_000_000, bytes_accessed=4_000_000, transcendentals=0),
        name="near_sums",
    )(got, mid, sig)


def sweeps_kernel(
    far_ref, near_ref, mid_ref, before_ref, after_ref, sig_ref, from_ref, back_ref,
    diag_scr, y_scr, p_scr, keep_scr, sol_scr, row_scr, place_scr, place_sem,
):
    to_scalar = pltpu.make_async_copy(from_ref, place_scr, place_sem)
    to_scalar.start()

    def put(scr, s, half, tile, value):
        scr[s + 2, half, tile * 8 : tile * 8 + 8, :] = value

    def get(scr, s, half, tile):
        return scr[s + 2, half, tile * 8 : tile * 8 + 8, :]

    def apply(scr, s, kind):
        near = beside([[get(scr, s, half, tile) for tile in range(TILES)] for half in range(2)])
        for half in range(2):
            for tile in range(TILES):
                here = get(scr, s, half, tile)
                beyond = get(scr, s - 1, half, tile) + get(scr, s + 1, half, tile)
                diag = diag_scr[kind, s + 1, half, tile * 8 : tile * 8 + 8, :]
                yield half, tile, here, diag * here - (beyond + near[half][tile])

    for half in range(2):
        for tile in range(TILES):
            nodes = slice(tile * 8, tile * 8 + 8)
            at = ROW + tile // 3 * 8
            for s in range(-1, 5):
                if 0 <= s < 4:
                    sigma = sig_ref[nodes, spot(s, half)]
                else:
                    sigma = (before_ref if s < 0 else after_ref)[at : at + 8, spot(tile % 3, half)]
                for i, mass in enumerate((mass_scale[0], mass_scale[3])):
                    diag_scr[i, s + 1, half, nodes, :] = 6.0 + mass * sigma

    def channel_step(channel, _):
        scalar = channel == 3
        invert, one, two, _ = [
            jnp.where(scalar, b, a).astype(F32) for a, b in zip(numbers(False), numbers(True))
        ]
        kind = jnp.where(scalar, 1, 0)
        base = channel * NODES
        across = two * invert

        def rows(tile):
            return pl.ds(pl.multiple_of(base + tile * 8, 8), 8)

        def source(s, half, tile):
            if s in (1, 2):
                return mid_ref[rows(tile), spot(s - 1, half)]
            ref = {-1: before_ref, 0: far_ref, 3: near_ref, 4: after_ref}[s]
            return ref[rows(tile), spot(0, half)]

        for half in range(2):
            for tile in range(TILES):
                for s, ref, beyond in ((0, far_ref, -1), (3, near_ref, 4), (-1, before_ref, 0), (4, after_ref, 3)):
                    part = ref[rows(tile), spot(1, half)]
                    put(y_scr, s, half, tile, part + across * source(beyond, half, tile))
                for s, ref in ((1, far_ref), (2, near_ref), (-2, before_ref), (5, after_ref)):
                    put(y_scr, s, half, tile, ref[rows(tile), spot(2, half)])
        for s in range(-1, 5):
            for half, tile, here, applied in apply(y_scr, s, kind):
                rest = source(s, half, tile) - applied
                put(p_scr, s, half, tile, rest * invert)
                if 0 <= s < 4:
                    keep_scr[s, half, tile * 8 : tile * 8 + 8, :] = rest
        for s in range(4):
            for half, tile, here, applied in apply(p_scr, s, kind):
                rest = keep_scr[s, half, tile * 8 : tile * 8 + 8, :] - applied
                value = (get(y_scr, s, half, tile) + here) + (one * here + two * rest)
                sol_scr[rows(tile), spot(s, half)] = value
        return 0

    lax.fori_loop(0, 4, channel_step, 0)
    for group in range(BLOCKS // 128):
        part = slice(group * 128, (group + 1) * 128)
        row_scr[part, :] = sol_scr[:, part].T
    to_scalar.wait()
    for slot in range(SLOTS):
        back_ref[slot : slot + 1, :] = row_scr[pl.ds(place_scr[slot // 128, slot % 128], 1), :]


def sweeps(far, near, mid, before, after, sig, labels):
    vmem = pl.BlockSpec(memory_space=pltpu.VMEM)
    field = pltpu.VMEM((8, 2, NODES, 128), F32)
    return pl.pallas_call(
        sweeps_kernel,
        out_shape=jax.ShapeDtypeStruct((SLOTS, ROW), F32),
        in_specs=[vmem] * 7,
        out_specs=vmem,
        scratch_shapes=[
            pltpu.VMEM((2, 6, 2, NODES, 128), F32),
            field,
            field,
            pltpu.VMEM((4, 2, NODES, 128), F32),
            pltpu.VMEM((ROW, BLOCKS), F32),
            pltpu.VMEM((BLOCKS, ROW), F32),
            pltpu.SMEM((SLOTS // 128, 128), I32),
            pltpu.SemaphoreType.DMA,
        ],
        compiler_params=pltpu.CompilerParams(vmem_limit_bytes=VMEM_LIMIT),
        name="sweeps",
    )(far, near, mid, before, after, sig, labels)


def lift_kernel(got_ref, slot_ref, res_ref, tan_ref, jac_ref, ends_ref, out_hbm, row_scr, y_scr, out_ref, out_sem):
    def take(group, step):
        for inner in range(16):
            block = group * 128 + step * 16 + inner
            row_scr[block : block + 1, :] = got_ref[pl.ds(slot_ref[0, block], 1), :]

    def turn(group):
        y_scr[group] = row_scr[group * 128 : (group + 1) * 128, :].T

    groups = BLOCKS // 128
    for step in range(8):
        take(0, step)
    turn(0)
    for group in range(groups):
        lanes = slice(group * 128, (group + 1) * 128)

        def pick(channel, low, quarter):
            parts = [
                jnp.take_along_axis(y_scr[group, channel * NODES + 8 * k : channel * NODES + 8 * k + 8, :], low, axis=0)
                for k in range(4)
            ]
            return jnp.where(
                quarter < 2,
                jnp.where(quarter == 0, parts[0], parts[1]),
                jnp.where(quarter == 2, parts[2], parts[3]),
            )

        for step in range(EDGES // 8):
            if group + 1 < groups:
                take(group + 1, step)
            edges = slice(step * 8, (step + 1) * 8)
            tail = ends_ref[0, edges, lanes]
            head = ends_ref[1, edges, lanes]
            tail_at = (tail & 7, tail >> 3)
            head_at = (head & 7, head >> 3)
            total = pick(3, *head_at) - pick(3, *tail_at)
            for channel in range(3):
                pair = pick(channel, *head_at) + pick(channel, *tail_at)
                total = total + 0.5 * tan_ref[channel, edges, lanes] * pair
            out_ref[edges, lanes] = jac_ref[edges, lanes] * res_ref[edges, lanes] + total
        if group + 1 < groups:
            turn(group + 1)
        pltpu.make_async_copy(out_ref.at[:, lanes], out_hbm.at[:, lanes], out_sem.at[group]).start()
    for group in range(groups):
        lanes = slice(group * 128, (group + 1) * 128)
        pltpu.make_async_copy(out_ref.at[:, lanes], out_hbm.at[:, lanes], out_sem.at[group]).wait()


def lift(got, slots, residual, tangent, jacobi, ends):
    vmem = pl.BlockSpec(memory_space=pltpu.VMEM)
    return pl.pallas_call(
        lift_kernel,
        out_shape=jax.ShapeDtypeStruct((EDGES, BLOCKS), F32),
        in_specs=[vmem, pl.BlockSpec(memory_space=pltpu.SMEM), vmem, vmem, vmem, vmem],
        out_specs=pl.BlockSpec(memory_space=pltpu.HBM),
        scratch_shapes=[
            pltpu.VMEM((BLOCKS, ROW), F32),
            pltpu.VMEM((BLOCKS // 128, ROW, 128), F32),
            pltpu.VMEM((EDGES, BLOCKS), F32),
            pltpu.SemaphoreType.DMA((BLOCKS // 128,)),
        ],
        compiler_params=pltpu.CompilerParams(vmem_limit_bytes=VMEM_LIMIT),
        name="lift",
    )(got, slots, residual, tangent, jacobi, ends)


def exchange(rows):
    parts = rows.reshape(DEVICES, CAP, ROW)
    return lax.all_to_all(parts, RING, split_axis=0, concat_axis=0, tiled=True).reshape(SLOTS, ROW)


def per_device(residual, tangent, jacobi, ends, target, node_block, sigma):
    slabs = range(DEVICES)
    between = [(place(s), place((s + 1 if s % 2 else s - 1) % DEVICES)) for s in slabs]
    within = [(place(s), place(s ^ 1)) for s in slabs]
    sig_own = lax.ppermute(sigma, RING, [(s, place(s)) for s in slabs])
    send, slots = edge_terms(
        residual, tangent, ends, target.reshape(1, BLOCKS), node_block.reshape(1, BLOCKS)
    )
    got = exchange(send)
    far, mid, labels, sig = far_sums(got, sig_own)
    before = lax.ppermute(far, RING, between)
    near = near_sums(got, mid, sig)
    after = lax.ppermute(near, RING, within)
    back = sweeps(far, near, mid, before, after, sig, labels)
    mine = exchange(back)
    return lift(mine, slots, residual, tangent, jacobi, ends)


def solution(mesh):
    in_specs = (
        P(None, RING),
        P(None, None, RING),
        P(None, RING),
        P(None, None, RING),
        P(RING, None),
        P(RING),
        P(RING, None, None),
    )
    return jax.shard_map(
        per_device, mesh=mesh, in_specs=in_specs, out_specs=P(None, RING), check_vma=False
    )
```

```python
import jax
import jax.numpy as jnp
from jax import lax
from jax.experimental import pallas as pl
from jax.experimental.pallas import tpu as pltpu
from jax.sharding import PartitionSpec as P

F32 = jnp.float32
BF16 = jnp.bfloat16
I32 = jnp.int32

EDGES = 64
NODES = 32
ROW = 4 * NODES
BLOCKS = 1024
CAP = 16
DEVICES = 128
SLOTS = DEVICES * CAP
SLICE = 256
HALO = 3 * SLICE
LABEL = 3 * NODES
RING = ("edge", "node")
VMEM_LIMIT = 24 * 1024 * 1024
FIRST_LIMIT = 60 * 1024 * 1024
MESSAGE = ROW + 16
TILES = NODES // 8

mass_scale = (1.0, 1.0, 1.0, 0.5)


def chebyshev_numbers(scale):
    upper = 12.0 + 8.0 * scale
    lower = upper / 8.0
    centre = (upper + lower) / 2.0
    radius = (upper - lower) / 2.0
    ratio = centre / radius
    first = 1.0 / ratio
    second = 1.0 / (2.0 * ratio - first)
    return (centre, second * first, 2.0 * second / radius)


def place(slab):
    return slab ^ (24 * ((slab >> 5) & 1)) ^ (6 * ((slab >> 3) & 1))


def odd_slab():
    return lax.axis_index("node") & 1


def split(value):
    high = value.astype(BF16)
    return high, (value - high.astype(F32)).astype(BF16)


def one_hot(mask):
    return jnp.where(mask, 1.0, 0.0).astype(BF16)


def iota(shape, dim):
    return lax.broadcasted_iota(I32, shape, dim)


def dot(left, right, dims):
    return lax.dot_general(left, right, (dims, ((), ())), preferred_element_type=F32)


def terms_kernel(
    target_hbm, block_hbm, res_hbm, tan_hbm, ends_hbm, send_hbm, slot_hbm,
    target_scr, block_scr, res_scr, tan_scr, ends_scr, term_scr, acc_scr, row_scr, send_scr, slot_ref, label_scr, place_scr,
    place_sem, list_sem, in_sem, out_sem,
):
    groups = BLOCKS // 128

    chunks = ((0, 128), (128, 128), (256, BLOCKS - 256))

    def fetch(chunk):
        lanes = pl.ds(*chunks[chunk])
        return [
            pltpu.make_async_copy(hbm.at[..., lanes], scr.at[..., lanes], in_sem.at[i, chunk])
            for i, (hbm, scr) in enumerate(((ends_hbm, ends_scr), (res_hbm, res_scr), (tan_hbm, tan_scr)))
        ]

    lists = [
        pltpu.make_async_copy(target_hbm, target_scr, list_sem.at[0]),
        pltpu.make_async_copy(block_hbm, block_scr, list_sem.at[1]),
    ]
    fetched = [fetch(chunk) for chunk in range(3)]
    for copy in fetched[0] + lists + fetched[1] + fetched[2]:
        copy.start()
    send_scr[...] = jnp.zeros((SLOTS, ROW), F32)
    node = iota((NODES, 128), 0)

    def turn(group):
        lanes = pl.ds(pl.multiple_of(group * 128, 128), 128)
        acc_scr[group, LABEL : LABEL + 1, :] = label_scr[:, lanes]
        row_scr[lanes, :] = acc_scr[group].T

    def post(group, step):
        for inner in range(16):
            block = group * 128 + step * 16 + inner
            send_scr[pl.ds(place_scr[0, block], 1), :] = row_scr[pl.ds(block, 1), :]

    def edge_step(step, lanes, sums):
        sums = list(sums)
        for inner in range(8):
            row = slice(inner, inner + 1)
            head = ends_scr[1, step, row, lanes] == node
            tail = ends_scr[0, step, row, lanes] == node
            either = head | tail
            value = res_scr[step, row, lanes]
            for channel in range(3):
                term = term_scr[channel, step, row, :]
                sums[channel] = sums[channel] + jnp.where(either, term, 0.0)
            sums[3] = sums[3] + jnp.where(head, value, jnp.where(tail, -value, 0.0))
        return tuple(sums)

    def lanes_step(group, turned, posted):
        lanes = pl.ds(pl.multiple_of(group * 128, 128), 128)
        term_scr[...] = 0.5 * tan_scr[:, :, :, lanes] * res_scr[:, :, lanes][None]
        if turned:
            turn(group - 1)
        sums = (jnp.zeros((NODES, 128), F32),) * 4
        for step in range(3):
            if posted:
                post(group - 2, step)
            sums = edge_step(step, lanes, sums)

        def tile_step(step, sums):
            if posted:
                post(group - 2, step)
            return edge_step(step, lanes, sums)

        sums = lax.fori_loop(3, EDGES // 8, tile_step, sums)
        for channel in range(3):
            acc_scr[group, channel * NODES : (channel + 1) * NODES, :] = sums[channel]
        acc_scr[group, LABEL:, :] = sums[3]

    for copy in fetched[0]:
        copy.wait()
    lanes_step(0, False, False)
    for copy in lists:
        copy.wait()

    holder = place(target_scr[...])
    device = iota((DEVICES, 128), 0)
    before = one_hot(iota((128, 128), 0) < iota((128, 128), 1))
    seen = jnp.zeros((DEVICES, 1), F32)
    for group in range(groups):
        lanes = slice(group * 128, (group + 1) * 128)
        same = holder[:, lanes] == device
        hot = jnp.where(same, 1.0, 0.0)
        count = dot(hot.astype(BF16), before, ((1,), (0,))) + seen
        rank = jnp.sum(jnp.where(same, count, 0.0), axis=0, keepdims=True)
        slot_ref[:, lanes] = holder[:, lanes] * CAP + rank.astype(I32)
        seen = seen + jnp.sum(hot, axis=1, keepdims=True)
    to_scalar = pltpu.make_async_copy(slot_ref, place_scr, place_sem.at[0])
    to_scalar.start()
    to_lift = pltpu.make_async_copy(slot_ref, slot_hbm, place_sem.at[1])
    to_lift.start()

    number = block_scr[...]
    label = (number & ~255) + (number & 7) * 32 + ((number >> 3) & 31)
    label = (label + 1).astype(F32)
    label_scr[...] = label

    for copy in fetched[1]:
        copy.wait()
    lanes_step(1, True, False)
    for copy in fetched[2]:
        copy.wait()
    to_scalar.wait()

    def group_step(group, _):
        lanes_step(group, True, True)
        return 0

    lax.fori_loop(2, groups, group_step, 0)
    turn(groups - 1)
    for group in (groups - 2, groups - 1):
        for step in range(8):
            post(group, step)
    parts = 8
    out = []
    for part in range(parts):
        rows = pl.ds(part * (SLOTS // parts), SLOTS // parts)
        out.append(pltpu.make_async_copy(send_scr.at[rows, :], send_hbm.at[rows, :], out_sem.at[part]))
    for copy in out:
        copy.start()
    for copy in out:
        copy.wait()
    to_lift.wait()


def edge_terms(residual, tangent, ends, target, node_block):
    tiles = EDGES // 8
    hbm = pl.BlockSpec(memory_space=pltpu.HBM)
    return pl.pallas_call(
        terms_kernel,
        out_shape=(
            jax.ShapeDtypeStruct((SLOTS, ROW), F32),
            jax.ShapeDtypeStruct((1, BLOCKS), I32),
        ),
        in_specs=[hbm] * 5,
        out_specs=[hbm, hbm],
        scratch_shapes=[
            pltpu.VMEM((1, BLOCKS), I32),
            pltpu.VMEM((1, BLOCKS), I32),
            pltpu.VMEM((tiles, 8, BLOCKS), F32),
            pltpu.VMEM((3, tiles, 8, BLOCKS), F32),
            pltpu.VMEM((2, tiles, 8, BLOCKS), I32),
            pltpu.VMEM((3, tiles, 8, 128), F32),
            pltpu.VMEM((BLOCKS // 128, ROW, 128), F32),
            pltpu.VMEM((BLOCKS, ROW), F32),
            pltpu.VMEM((SLOTS, ROW), F32),
            pltpu.VMEM((1, BLOCKS), I32),
            pltpu.VMEM((1, BLOCKS), F32),
            pltpu.SMEM((1, BLOCKS), I32),
            pltpu.SemaphoreType.DMA((2,)),
            pltpu.SemaphoreType.DMA((2,)),
            pltpu.SemaphoreType.DMA((3, 3)),
            pltpu.SemaphoreType.DMA((8,)),
        ],
        compiler_params=pltpu.CompilerParams(vmem_limit_bytes=FIRST_LIMIT),
        cost_estimate=pl.CostEstimate(flops=50_000_000, bytes_accessed=20_000_000, transcendentals=0),
        name="edge_terms",
    )(
        target,
        node_block,
        residual.reshape(tiles, 8, BLOCKS),
        tangent.reshape(3, tiles, 8, BLOCKS),
        ends.reshape(2, tiles, 8, BLOCKS),
    )


def numbers(scalar):
    centre, one, two = chebyshev_numbers(mass_scale[3 if scalar else 0])
    return 1.0 / centre, one, two, mass_scale[3 if scalar else 0]


def beside(here):
    lane = iota((8, 128), 1)
    row = iota((8, 128), 0)
    low, high = (lane & 31) > 0, (lane & 31) < 31
    bottom, top = row == 0, row == 7
    up = [[pltpu.roll(value, 1, 0) for value in part] for part in here]
    down = [[pltpu.roll(value, 7, 0) for value in part] for part in here]
    first = [pltpu.roll(part[-1], 32, 1) for part in up]
    last = [pltpu.roll(part[0], 96, 1) for part in down]
    first = [jnp.where(lane < 32, 0.0, first[0]), jnp.where(lane < 32, first[0], first[1])]
    last = [jnp.where(lane < 96, last[0], last[1]), jnp.where(lane < 96, last[1], 0.0)]
    sums = []
    for half in range(2):
        sums.append([])
        for tile in range(TILES):
            below = up[half][tile - 1] if tile else first[half]
            above = down[half][tile + 1] if tile < TILES - 1 else last[half]
            axial = jnp.where(bottom, below, up[half][tile]) + jnp.where(top, above, down[half][tile])
            value = here[half][tile]
            inner = jnp.where(low, pltpu.roll(value, 1, 1), 0.0)
            outer = jnp.where(high, pltpu.roll(value, 127, 1), 0.0)
            sums[half].append((axial + inner) + outer)
    return sums


def spot(s, half):
    return slice(s * SLICE + half * 128, s * SLICE + half * 128 + 128)


def summed(rows_scr, hot):
    both = dot(rows_scr[...], hot, ((1,), (0,)))
    sums = both[:ROW] + both[ROW:]
    first = iota((NODES, SLICE), 0) == 0
    scalar = sums[LABEL:]
    rest = -jnp.sum(jnp.where(first, 0.0, scalar), axis=0, keepdims=True)
    return jnp.concatenate([sums[:LABEL], jnp.where(first, rest, scalar)], axis=0)


def turned_label(label):
    return (label.astype(I32) - 1) ^ (odd_slab() * 768)


def first_sweep(source, sigma, store, s, inside):
    for channel in range(4):
        invert, one, two, mass = numbers(channel == 3)
        here = [
            [source(channel, s, half, tile) * invert for tile in range(TILES)] for half in range(2)
        ]
        near = beside(here)
        for half in range(2):
            for tile in range(TILES):
                around = near[half][tile]
                for other in inside:
                    around = around + source(channel, other, half, tile) * invert
                value = here[half][tile]
                rest = source(channel, s, half, tile) - (
                    (6.0 + mass * sigma(s, half, tile)) * value - around
                )
                store(channel, half, tile, value + (one * value + two * rest))


def put_sigma(message_ref, sig_ref, s):
    for tile in range(TILES):
        at, lanes = ROW + tile // 3 * 8, slice(tile % 3 * SLICE, (tile % 3 + 1) * SLICE)
        message_ref[at : at + 8, lanes] = sig_ref[tile * 8 : tile * 8 + 8, s * SLICE : (s + 1) * SLICE]
    message_ref[ROW + 8 :, SLICE:] = jnp.zeros((8, 2 * SLICE), F32)


def channel_rows(channel, tile):
    at = channel * NODES + tile * 8
    return slice(at, at + 8)


def far_kernel(got_ref, sigma_ref, far_ref, mid_ref, from_ref, sig_ref, rows_scr, hot_scr):
    for s in range(4):
        turned = sigma_ref[s ^ (odd_slab() * 3)].T
        for block in range(8):
            at = s * SLICE + block * 32
            sig_ref[:, at : at + 32] = turned[block * 32 : (block + 1) * 32, :]
    for step in range(SLOTS // 128):
        part = slice(step * 128, (step + 1) * 128)
        turned = got_ref[part, :].T
        high, low = split(turned)
        rows_scr[0:ROW, part] = high
        rows_scr[ROW:, part] = low
        from_ref[step : step + 1, :] = jnp.maximum(turned_label(turned[LABEL : LABEL + 1, :]), 0)
        column = turned_label(got_ref[part, LABEL : LABEL + 1])
        hot_scr[part, :] = one_hot(column == iota((128, HALO), 1))

    def source(channel, s, half, tile):
        if s == 0:
            return far_ref[channel_rows(channel, tile), spot(0, half)]
        return mid_ref[channel_rows(channel, tile), spot(s - 1, half)]

    def sigma(s, half, tile):
        return sig_ref[tile * 8 : tile * 8 + 8, spot(s, half)]

    def store(s):
        def one(channel, half, tile, value):
            far_ref[channel_rows(channel, tile), spot(1 + s, half)] = value

        return one

    for s in range(3):
        sums = summed(rows_scr, hot_scr[:, s * SLICE : (s + 1) * SLICE])
        if s == 0:
            far_ref[0:ROW, 0:SLICE] = sums
        else:
            mid_ref[:, (s - 1) * SLICE : s * SLICE] = sums
    first_sweep(source, sigma, store(0), 0, (1,))
    first_sweep(source, sigma, store(1), 1, (0, 2))
    put_sigma(far_ref, sig_ref, 0)


def far_sums(got, sigma):
    vmem = pl.BlockSpec(memory_space=pltpu.VMEM)
    return pl.pallas_call(
        far_kernel,
        out_shape=(
            jax.ShapeDtypeStruct((MESSAGE, HALO), F32),
            jax.ShapeDtypeStruct((ROW, 2 * SLICE), F32),
            jax.ShapeDtypeStruct((SLOTS // 128, 128), I32),
            jax.ShapeDtypeStruct((NODES, BLOCKS), F32),
        ),
        in_specs=[vmem] * 2,
        out_specs=[vmem] * 4,
        scratch_shapes=[
            pltpu.VMEM((2 * ROW, SLOTS), BF16),
            pltpu.VMEM((SLOTS, HALO), BF16),
        ],
        compiler_params=pltpu.CompilerParams(vmem_limit_bytes=VMEM_LIMIT),
        cost_estimate=pl.CostEstimate(flops=800_000_000, bytes_accessed=5_000_000, transcendentals=0),
        name="far_sums",
    )(got, sigma)


def near_kernel(got_ref, mid_ref, sig_ref, near_ref, rows_scr, hot_scr):
    for step in range(SLOTS // 128):
        part = slice(step * 128, (step + 1) * 128)
        high, low = split(got_ref[part, :].T)
        rows_scr[0:ROW, part] = high
        rows_scr[ROW:, part] = low
        column = turned_label(got_ref[part, LABEL : LABEL + 1])
        hot_scr[part, :] = one_hot(column == iota((128, SLICE), 1) + HALO)

    def source(channel, s, half, tile):
        if s == 3:
            return near_ref[channel_rows(channel, tile), spot(0, half)]
        return mid_ref[channel_rows(channel, tile), spot(s - 1, half)]

    def sigma(s, half, tile):
        return sig_ref[tile * 8 : tile * 8 + 8, spot(s, half)]

    def store(s):
        def one(channel, half, tile, value):
            near_ref[channel_rows(channel, tile), spot(4 - s, half)] = value

        return one

    near_ref[0:ROW, 0:SLICE] = summed(rows_scr, hot_scr[...])
    first_sweep(source, sigma, store(3), 3, (2,))
    first_sweep(source, sigma, store(2), 2, (1, 3))
    put_sigma(near_ref, sig_ref, 3)


def near_sums(got, mid, sig):
    vmem = pl.BlockSpec(memory_space=pltpu.VMEM)
    return pl.pallas_call(
        near_kernel,
        out_shape=jax.ShapeDtypeStruct((MESSAGE, HALO), F32),
        in_specs=[vmem] * 3,
        out_specs=vmem,
        scratch_shapes=[
            pltpu.VMEM((2 * ROW, SLOTS), BF16),
            pltpu.VMEM((SLOTS, SLICE), BF16),
        ],
        compiler_params=pltpu.CompilerParams(vmem_limit_bytes=VMEM_LIMIT),
        cost_estimate=pl.CostEstimate(flops=300_000_000, bytes_accessed=4_000_000, transcendentals=0),
        name="near_sums",
    )(got, mid, sig)


def sweeps_kernel(
    far_ref, near_ref, mid_ref, before_ref, after_ref, sig_ref, from_ref, back_ref,
    diag_scr, y_scr, p_scr, keep_scr, sol_scr, row_scr, place_scr, place_sem,
):
    to_scalar = pltpu.make_async_copy(from_ref, place_scr, place_sem)
    to_scalar.start()

    def put(scr, s, half, tile, value):
        scr[s + 2, half, tile * 8 : tile * 8 + 8, :] = value

    def get(scr, s, half, tile):
        return scr[s + 2, half, tile * 8 : tile * 8 + 8, :]

    def apply(scr, s, kind):
        near = beside([[get(scr, s, half, tile) for tile in range(TILES)] for half in range(2)])
        for half in range(2):
            for tile in range(TILES):
                here = get(scr, s, half, tile)
                beyond = get(scr, s - 1, half, tile) + get(scr, s + 1, half, tile)
                diag = diag_scr[kind, s + 1, half, tile * 8 : tile * 8 + 8, :]
                yield half, tile, here, diag * here - (beyond + near[half][tile])

    for half in range(2):
        for tile in range(TILES):
            nodes = slice(tile * 8, tile * 8 + 8)
            at = ROW + tile // 3 * 8
            for s in range(-1, 5):
                if 0 <= s < 4:
                    sigma = sig_ref[nodes, spot(s, half)]
                else:
                    sigma = (before_ref if s < 0 else after_ref)[at : at + 8, spot(tile % 3, half)]
                for i, mass in enumerate((mass_scale[0], mass_scale[3])):
                    diag_scr[i, s + 1, half, nodes, :] = 6.0 + mass * sigma

    def channel_step(channel, _):
        scalar = channel == 3
        invert, one, two, _ = [
            jnp.where(scalar, b, a).astype(F32) for a, b in zip(numbers(False), numbers(True))
        ]
        kind = jnp.where(scalar, 1, 0)
        base = channel * NODES
        across = two * invert

        def rows(tile):
            return pl.ds(pl.multiple_of(base + tile * 8, 8), 8)

        def source(s, half, tile):
            if s in (1, 2):
                return mid_ref[rows(tile), spot(s - 1, half)]
            ref = {-1: before_ref, 0: far_ref, 3: near_ref, 4: after_ref}[s]
            return ref[rows(tile), spot(0, half)]

        for half in range(2):
            for tile in range(TILES):
                for s, ref, beyond in ((0, far_ref, -1), (3, near_ref, 4), (-1, before_ref, 0), (4, after_ref, 3)):
                    part = ref[rows(tile), spot(1, half)]
                    put(y_scr, s, half, tile, part + across * source(beyond, half, tile))
                for s, ref in ((1, far_ref), (2, near_ref), (-2, before_ref), (5, after_ref)):
                    put(y_scr, s, half, tile, ref[rows(tile), spot(2, half)])
        for s in range(-1, 5):
            for half, tile, here, applied in apply(y_scr, s, kind):
                rest = source(s, half, tile) - applied
                put(p_scr, s, half, tile, rest * invert)
                if 0 <= s < 4:
                    keep_scr[s, half, tile * 8 : tile * 8 + 8, :] = rest
        for s in range(4):
            for half, tile, here, applied in apply(p_scr, s, kind):
                rest = keep_scr[s, half, tile * 8 : tile * 8 + 8, :] - applied
                value = (get(y_scr, s, half, tile) + here) + (one * here + two * rest)
                sol_scr[rows(tile), spot(s, half)] = value
        return 0

    lax.fori_loop(0, 4, channel_step, 0, unroll=2)
    for group in range(BLOCKS // 128):
        part = slice(group * 128, (group + 1) * 128)
        row_scr[part, :] = sol_scr[:, part].T
    to_scalar.wait()
    for slot in range(SLOTS):
        back_ref[slot : slot + 1, :] = row_scr[pl.ds(place_scr[slot // 128, slot % 128], 1), :]


def sweeps(far, near, mid, before, after, sig, labels):
    vmem = pl.BlockSpec(memory_space=pltpu.VMEM)
    field = pltpu.VMEM((8, 2, NODES, 128), F32)
    return pl.pallas_call(
        sweeps_kernel,
        out_shape=jax.ShapeDtypeStruct((SLOTS, ROW), F32),
        in_specs=[vmem] * 7,
        out_specs=vmem,
        scratch_shapes=[
            pltpu.VMEM((2, 6, 2, NODES, 128), F32),
            field,
            field,
            pltpu.VMEM((4, 2, NODES, 128), F32),
            pltpu.VMEM((ROW, BLOCKS), F32),
            pltpu.VMEM((BLOCKS, ROW), F32),
            pltpu.SMEM((SLOTS // 128, 128), I32),
            pltpu.SemaphoreType.DMA,
        ],
        compiler_params=pltpu.CompilerParams(vmem_limit_bytes=VMEM_LIMIT),
        name="sweeps",
    )(far, near, mid, before, after, sig, labels)


def lift_kernel(got_ref, slot_ref, res_ref, tan_ref, jac_ref, ends_ref, out_hbm, row_scr, y_scr, out_ref, out_sem):
    def take(group, step):
        for inner in range(16):
            block = group * 128 + step * 16 + inner
            row_scr[block : block + 1, :] = got_ref[pl.ds(slot_ref[0, block], 1), :]

    def turn(group):
        y_scr[group] = row_scr[group * 128 : (group + 1) * 128, :].T

    groups = BLOCKS // 128
    for step in range(8):
        take(0, step)
    turn(0)
    for group in range(groups):
        lanes = slice(group * 128, (group + 1) * 128)

        def pick(channel, low, quarter):
            parts = [
                jnp.take_along_axis(y_scr[group, channel * NODES + 8 * k : channel * NODES + 8 * k + 8, :], low, axis=0)
                for k in range(4)
            ]
            return jnp.where(
                quarter < 2,
                jnp.where(quarter == 0, parts[0], parts[1]),
                jnp.where(quarter == 2, parts[2], parts[3]),
            )

        for step in range(EDGES // 8):
            if group + 1 < groups:
                take(group + 1, step)
            edges = slice(step * 8, (step + 1) * 8)
            tail = ends_ref[0, edges, lanes]
            head = ends_ref[1, edges, lanes]
            tail_at = (tail & 7, tail >> 3)
            head_at = (head & 7, head >> 3)
            total = pick(3, *head_at) - pick(3, *tail_at)
            for channel in range(3):
                pair = pick(channel, *head_at) + pick(channel, *tail_at)
                total = total + 0.5 * tan_ref[channel, edges, lanes] * pair
            out_ref[edges, lanes] = jac_ref[edges, lanes] * res_ref[edges, lanes] + total
        if group + 1 < groups:
            turn(group + 1)
        pltpu.make_async_copy(out_ref.at[:, lanes], out_hbm.at[:, lanes], out_sem.at[group]).start()
    for group in range(groups):
        lanes = slice(group * 128, (group + 1) * 128)
        pltpu.make_async_copy(out_ref.at[:, lanes], out_hbm.at[:, lanes], out_sem.at[group]).wait()


def lift(got, slots, residual, tangent, jacobi, ends):
    vmem = pl.BlockSpec(memory_space=pltpu.VMEM)
    return pl.pallas_call(
        lift_kernel,
        out_shape=jax.ShapeDtypeStruct((EDGES, BLOCKS), F32),
        in_specs=[vmem, pl.BlockSpec(memory_space=pltpu.SMEM), vmem, vmem, vmem, vmem],
        out_specs=pl.BlockSpec(memory_space=pltpu.HBM),
        scratch_shapes=[
            pltpu.VMEM((BLOCKS, ROW), F32),
            pltpu.VMEM((BLOCKS // 128, ROW, 128), F32),
            pltpu.VMEM((EDGES, BLOCKS), F32),
            pltpu.SemaphoreType.DMA((BLOCKS // 128,)),
        ],
        compiler_params=pltpu.CompilerParams(vmem_limit_bytes=VMEM_LIMIT),
        name="lift",
    )(got, slots, residual, tangent, jacobi, ends)


def exchange(rows):
    parts = rows.reshape(DEVICES, CAP, ROW)
    return lax.all_to_all(parts, RING, split_axis=0, concat_axis=0, tiled=True).reshape(SLOTS, ROW)


def per_device(residual, tangent, jacobi, ends, target, node_block, sigma):
    slabs = range(DEVICES)
    between = [(place(s), place((s + 1 if s % 2 else s - 1) % DEVICES)) for s in slabs]
    within = [(place(s), place(s ^ 1)) for s in slabs]
    sig_own = lax.ppermute(sigma, RING, [(s, place(s)) for s in slabs])
    send, slots = edge_terms(
        residual, tangent, ends, target.reshape(1, BLOCKS), node_block.reshape(1, BLOCKS)
    )
    got = exchange(send)
    far, mid, labels, sig = far_sums(got, sig_own)
    before = lax.ppermute(far, RING, between)
    near = near_sums(got, mid, sig)
    after = lax.ppermute(near, RING, within)
    back = sweeps(far, near, mid, before, after, sig, labels)
    mine = exchange(back)
    return lift(mine, slots, residual, tangent, jacobi, ends)


def solution(mesh):
    in_specs = (
        P(None, RING),
        P(None, None, RING),
        P(None, RING),
        P(None, None, RING),
        P(RING, None),
        P(RING),
        P(RING, None, None),
    )
    return jax.shard_map(
        per_device, mesh=mesh, in_specs=in_specs, out_specs=P(None, RING), check_vma=False
    )
```
